32 devices in a mesh: dp: 8 (over z, y), tensor: 4 (over x, core).
Axes of the slice: x: 2, y: 2, z: 4, core: 2. Of those that a mesh axis runs over, the one named last changes fastest.
Arguments:
- layer_input: bfloat16 [16384, 1536], P('dp'), may hold values from -6 to 6
- segments: int32 [16384], P('dp'), may hold values from 0 to 2048, as said below
- routes: int32 [16384, 8], P(('dp', 'tensor')), may hold values from 0 to 31, all different within a row; in each aligned block of 512 rows (0 to 511, 512 to 1023, ...) at most 160 rows name the same one
- norm1_gain: bfloat16 [1536], replicated, may hold values from 0.5 to 1.5
- w_query: bfloat16 [1536, 1536], P(None, 'tensor'), may hold values from -0.15625 to 0.15625
- w_key: bfloat16 [1536, 512], P(None, 'tensor'), may hold values from -0.15625 to 0.15625
- w_value: bfloat16 [1536, 512], P(None, 'tensor'), may hold values from -0.15625 to 0.15625
- w_output: bfloat16 [1536, 1536], P('tensor'), may hold values from -2.5 to 2.5
- norm2_gain: bfloat16 [1536], replicated, may hold values from 0.5 to 1.5
- router: bfloat16 [1536, 32], replicated, may hold values from -0.078125 to 0.078125
- w_gate: bfloat16 [32, 1536, 512], P('dp'), may hold values from -0.15625 to 0.15625
- w_up: bfloat16 [32, 1536, 512], P('dp'), may hold values from -0.15625 to 0.15625
- w_down: bfloat16 [32, 512, 1536], P('dp'), may hold values from -0.75 to 0.75
- cotangent: bfloat16 [16384, 1536], P(('dp', 'tensor')), may hold values from -6 to 6
Outputs:
- layer_out: bfloat16 [16384, 1536], P(('dp', 'tensor'))
- input_grad: float32 [16384, 1536], P(('dp', 'tensor'))
- norm1_grad: float32 [1536], P(('dp', 'tensor'))
- query_grad: float32 [1536, 1536], P('dp', 'tensor')
- key_grad: float32 [1536, 512], P('dp', 'tensor')
- value_grad: float32 [1536, 512], P('dp', 'tensor')
- output_grad: float32 [1536, 1536], P('tensor', 'dp')
- norm2_grad: float32 [1536], P(('dp', 'tensor'))
- router_grad: float32 [1536, 32], P(('dp', 'tensor'))
- gate_grad: float32 [32, 1536, 512], P('dp', 'tensor')
- up_grad: float32 [32, 1536, 512], P('dp', 'tensor')
- down_grad: float32 [32, 512, 1536], P('dp', None, 'tensor')
The draws below stay inside these ranges and needn't reach their ends.
Inputs may be any that keep to these rules, and one draw needn't show every extreme that they name: `segments`: within each sequence of 2048 tokens the numbers never fall until its last 1 to 256 tokens, which are 0; 0 appears nowhere else. In each sequence the last document before the padding is numbered 2048. `routes`: each token names 8 different experts. Among the 512 tokens of one device (aligned blocks of rows) no expert is named more than 160 times, a bound that some block reaches.
All inputs are finite; a program needn't handle non-finite values.
Results may differ from the reference program's by a relative error of at most 0.025.
Values may be sent and summed in bfloat16 or wider, within the bound.
No kernel may reach another device: no remote copies, remote signals or barrier semaphores. Data moves between devices by JAX's collectives and lax.ppermute only.
A program may use at most 384 MiB of HBM per device.

```python
import math
import jax
import jax.numpy as jnp
import numpy as np
from jax import lax

D = 1536
QH = 24
KVH = 8
HD = 64
FFE = 512
TOPK = 8
WINDOW = 1024
SEQ = 2048
EXPERTS = 32
TOK_DEV = 2048
TQ = 512
SEQS = 8
TOKENS = 16384
CAP = 160
N_TENSOR = 4


def draw_segments(key, part):
    key = jax.random.fold_in(key, 11)
    first_key, second_key = jax.random.split(key)
    breaks = (jax.random.randint(first_key, (SEQS, SEQ), 0, SEQ // 2) == 0).astype(jnp.int32)
    breaks = breaks.at[:, 0].set(0)
    doc_ids = 1 + jnp.cumsum(breaks, axis=1)
    padding = jax.random.randint(second_key, (SEQS, 1), 1, SEQ // 8 + 1)
    last_place = (SEQ - padding - 1).astype(jnp.int32)
    last_id = jnp.take_along_axis(doc_ids, last_place, axis=1)
    doc_ids = doc_ids + SEQ - last_id
    places = jnp.arange(SEQ, dtype=jnp.int32)[None, :]
    doc_ids = jnp.where(places >= SEQ - padding, 0, doc_ids)
    return doc_ids.reshape(-1).astype(jnp.int32)


def shard_levels(own_key, extent, pieces, smallest, largest):
    level, own = 1.0, jax.random.fold_in(own_key, 6)
    for axis_at, blocks in pieces:
        steps = jnp.exp(jax.random.uniform(jax.random.fold_in(own, axis_at), (blocks,), jnp.float32, smallest / len(pieces), largest / len(pieces)))
        level = level * jnp.repeat(steps, extent[axis_at] // blocks).reshape([-1 if axis == axis_at else 1 for axis in range(len(extent))])
    return level


def deal_out(key, own, number, rows, number_of, top, limit, lean):
    order = jax.random.permutation(key, number_of)
    crowded, usual = portions_of(number_of, rows * top, limit, lean, True), portions_of(number_of, rows * top, limit, lean, False)
    places = jnp.arange(number_of)

    def named(lengths, turn):
        used = int((lengths > 0).sum())
        fixed = max(1, used // 4)
        moved = fixed + (places - fixed + turn * (used - fixed)) % max(1, number_of - fixed)
        return jnp.zeros((number_of,), jnp.int32).at[order[jnp.where(places < fixed, places, moved)]].set(jnp.asarray(lengths, jnp.int32))

    lengths = jnp.where(number % 4 == 0, named(crowded, number // 4), named(usual, number - number // 4 - 1))
    mixed = jax.random.permutation(jax.random.fold_in(own, 3), number_of)
    giver, taker = mixed[0:number_of // 2 * 2:2], mixed[1:number_of // 2 * 2:2]
    slack = jnp.minimum(lengths[giver] - 1, limit - lengths[taker]) // 2
    slack = jnp.where((giver == order[0]) | (taker == order[0]) | (lengths[taker] == 0), 0, jnp.maximum(slack, 0))
    moved = jax.random.randint(jax.random.fold_in(own, 4), (number_of // 2,), 0, 1 << 20) % (slack + 1)
    lengths = lengths.at[giver].add(-moved).at[taker].add(moved)
    members = jnp.searchsorted(jnp.cumsum(lengths), jnp.arange(rows * top), side="right").astype(jnp.int32)
    listing = members.reshape(top, rows).T
    listing = listing[jax.random.permutation(jax.random.fold_in(own, 1), rows)]
    turn = jax.random.randint(jax.random.fold_in(own, 2), (rows, 1), 0, top)
    return jnp.take_along_axis(listing, (jnp.arange(top)[None, :] + turn) % top, axis=1)


def portions_of(count, total, most, skew, full):
    weights = [(1 << 20) // math.isqrt(grade ** skew) + 1 for grade in range(1, count + 1)]
    largest = most if full else min(most, max(-(-total // count), total * weights[0] // sum(weights)))
    least = 1 if total - largest >= count - 1 else 0
    holding, surplus = [largest] + [least] * (count - 1), total - largest - least * (count - 1)
    while surplus > 0:
        candidates = [i for i in range(1, count) if holding[i] < largest] or [i for i in range(1, count) if holding[i] < most]
        mass, left = sum([weights[i] for i in candidates]), surplus
        for i in candidates:
            extra = min(most - holding[i], max(1, left * weights[i] // mass), surplus)
            holding[i] = holding[i] + extra
            surplus = surplus - extra
    return np.array(holding)


def normal_values(stream_key, dims, deviation, limit, cuts=(), kind=jnp.bfloat16):
    values = jax.random.normal(stream_key, dims, jnp.float32) * deviation
    if len(cuts) > 0:
        values = shard_levels(stream_key, dims, cuts, -0.22, 0.18) * values
    return jnp.clip(values, min=-limit, max=limit).astype(kind)


def setup_inputs(seed: int = 0) -> dict:
    streams_of = jax.random.split(jax.random.key(seed), 15)
    layer_input = normal_values(streams_of[0], (TOKENS, D), 1.0, 6.0, ((0, 8),))
    segments = draw_segments(jax.random.fold_in(streams_of[14], 71), 0)
    routes_keys = jax.random.split(jax.random.fold_in(streams_of[2], 1), TOKENS // TQ)
    routes_turns = jax.random.permutation(jax.random.fold_in(streams_of[2], 3), TOKENS // TQ)
    routes = jax.vmap(lambda own, number: deal_out(jax.random.fold_in(streams_of[2], 2), own, number, TQ, EXPERTS, TOPK, CAP, 1))(routes_keys, routes_turns).reshape((TOKENS, TOPK))
    norm1_gain = jnp.clip(1.0 + 0.1 * jax.random.normal(streams_of[3], (D,), jnp.float32), 0.5, 1.5).astype(jnp.bfloat16)
    w_query = normal_values(streams_of[4], (D, QH * HD), D ** -0.5, 0.15625, ((1, 4),))
    w_key = normal_values(streams_of[5], (D, KVH * HD), D ** -0.5, 0.15625, ((1, 4),))
    w_value = normal_values(streams_of[6], (D, KVH * HD), D ** -0.5, 0.15625, ((1, 4),))
    w_output = normal_values(streams_of[7], (QH * HD, D), (max(1, QH * HD // 256)) ** -0.5, 2.5, ((0, 4),))
    norm2_gain = jnp.clip(1.0 + 0.1 * jax.random.normal(streams_of[8], (D,), jnp.float32), 0.5, 1.5).astype(jnp.bfloat16)
    router = normal_values(streams_of[9], (D, EXPERTS), (4 * D) ** -0.5, 0.078125)
    w_gate = normal_values(streams_of[10], (EXPERTS, D, FFE), D ** -0.5, 0.15625, ((0, 8),))
    w_up = normal_values(streams_of[11], (EXPERTS, D, FFE), D ** -0.5, 0.15625, ((0, 8),))
    w_down = normal_values(streams_of[12], (EXPERTS, FFE, D), (FFE // 8) ** -0.5, 0.75, ((0, 8),))
    cotangent = normal_values(streams_of[13], (TOKENS, D), 1.0, 6.0, ((0, 32),))
    return dict(layer_input=layer_input, segments=segments, routes=routes, norm1_gain=norm1_gain, w_query=w_query, w_key=w_key, w_value=w_value, w_output=w_output, norm2_gain=norm2_gain, router=router, w_gate=w_gate, w_up=w_up, w_down=w_down, cotangent=cotangent)


epsilon = 1e-05
highest = lax.Precision.HIGHEST

@jax.custom_vjp
def low(v):
    return lax.optimization_barrier(v.astype(jnp.bfloat16)).astype(jnp.float32)

@jax.custom_vjp
def low_back(v):
    return v

def low_keep(v):
    return (low(v), None)

def low_pass(kept, grad):
    return (grad,)

def back_keep(v):
    return (v, None)

def back_low(kept, grad):
    return (low(grad),)
low.defvjp(low_keep, low_pass)
low_back.defvjp(back_keep, back_low)

def rotate(values, places, direction):
    half_dim = values.shape[-1] // 2
    frequency = 10000.0 ** (-jnp.arange(half_dim).astype(jnp.float32) / half_dim)
    angles = places.astype(jnp.float32)[:, None] * frequency[None, :]
    cos_table = jnp.cos(angles)[:, None, :]
    sin_table = direction * jnp.sin(angles)[:, None, :]
    lower_half = values[..., :half_dim]
    upper_half = values[..., half_dim:]
    return jnp.concatenate([lower_half * cos_table - upper_half * sin_table, upper_half * cos_table + lower_half * sin_table], axis=-1)

def slot_tables(route_rows, experts, capacity):
    flat_routes = route_rows.reshape(-1).astype(jnp.int32)
    slot_count = flat_routes.shape[0]
    one_hot = (flat_routes[:, None] == jnp.arange(experts, dtype=jnp.int32)[None, :]).astype(jnp.int32)
    earlier = jnp.cumsum(one_hot, axis=0) - one_hot
    slot_rank = lax.optimization_barrier(jnp.sum(earlier * one_hot, axis=1))
    places = (flat_routes * capacity + slot_rank).astype(jnp.int32)
    filled = jnp.full((experts * capacity,), slot_count, jnp.int32).at[places].set(jnp.arange(slot_count, dtype=jnp.int32))
    return (places, filled)

def attend(q_rot, k_rot, v_low, seg_ids):
    length = q_rot.shape[0]
    block_rows = min(512, length)
    group_size = QH // KVH
    q_blocks = q_rot.reshape(length // block_rows, block_rows, KVH, group_size, HD)
    key_ids = jnp.arange(length, dtype=jnp.int32)

    def one_block(inputs):
        q_block, offset = inputs
        row_ids = offset + jnp.arange(block_rows, dtype=jnp.int32)
        row_seg = lax.dynamic_slice_in_dim(seg_ids, offset, block_rows)
        allowed = (key_ids[None, :] <= row_ids[:, None]) & (row_ids[:, None] - key_ids[None, :] < WINDOW)
        allowed = allowed & (seg_ids[None, :] == row_seg[:, None]) & (row_seg[:, None] != 0)
        allowed = allowed | (key_ids[None, :] == row_ids[:, None])
        scores = low_back(jnp.einsum('qgjd,kgd->gjqk', q_block, k_rot, precision=highest) * HD ** (-0.5))
        scores = jnp.where(allowed[None, None], scores, -jnp.inf)
        prob_rows = low(jax.nn.softmax(scores, axis=-1))
        return jnp.einsum('gjqk,kgd->qgjd', prob_rows, v_low, precision=highest)
    offsets = (jnp.arange(length // block_rows) * block_rows).astype(jnp.int32)
    head_out = lax.map(jax.checkpoint(one_block), (q_blocks, offsets))
    return head_out.reshape(length, QH * HD)

def attention_layer(seq_rows, seg_ids, first_gain, query_mat, key_mat, value_mat, out_mat):
    length = seq_rows.shape[0]
    inv_rms = lax.rsqrt(lax.optimization_barrier(jnp.mean(seq_rows * seq_rows, axis=-1, keepdims=True)) + epsilon)
    normed = low(seq_rows * inv_rms * first_gain)
    q_pre = low_back(jnp.dot(normed, query_mat, precision=highest)).reshape(length, QH, HD)
    k_pre = low_back(jnp.dot(normed, key_mat, precision=highest)).reshape(length, KVH, HD)
    v_pre = low_back(jnp.dot(normed, value_mat, precision=highest)).reshape(length, KVH, HD)
    places = jnp.arange(length, dtype=jnp.int32) % SEQ
    q_rot = low(rotate(q_pre, places, 1.0))
    k_rot = low(rotate(k_pre, places, 1.0))
    heads = attend(q_rot, k_rot, low(v_pre), seg_ids)
    heads = low(low_back(heads))
    return seq_rows + low_back(jnp.dot(heads, out_mat, precision=highest))

def expert_layer(mid_rows, route_rows, second_gain, router_mat, gate_mat, up_mat, down_mat):
    inv_rms = lax.rsqrt(lax.optimization_barrier(jnp.mean(mid_rows * mid_rows, axis=-1, keepdims=True)) + epsilon)
    normed = low(mid_rows * inv_rms * second_gain)
    logits = low_back(jnp.dot(normed, router_mat, precision=highest))
    mixing = jax.nn.softmax(jnp.take_along_axis(logits, route_rows, axis=1), axis=-1)
    places, filled = slot_tables(route_rows, EXPERTS, CAP)
    padded = jnp.concatenate([normed, jnp.zeros((1, D), jnp.float32)], axis=0)
    sent = low_back(jnp.take(padded, filled // TOPK, axis=0)).reshape(EXPERTS, CAP, D)
    gate_pre = low_back(jnp.einsum('ecd,edh->ech', sent, gate_mat, precision=highest))
    up_pre = low_back(jnp.einsum('ecd,edh->ech', sent, up_mat, precision=highest))
    hidden_act = low(jax.nn.silu(gate_pre) * up_pre)
    expert_out = low(low_back(jnp.einsum('ech,ehd->ecd', hidden_act, down_mat, precision=highest))).reshape(EXPERTS * CAP, D)
    picked = jnp.take(expert_out, places, axis=0).reshape(-1, TOPK, D)
    return mid_rows + lax.optimization_barrier(jnp.sum(mixing[:, :, None] * picked, axis=1))

def reference(layer_input, segments, routes, norm1_gain, w_query, w_key, w_value, w_output, norm2_gain, router, w_gate, w_up, w_down, cotangent):
    token_rows = TOK_DEV // N_TENSOR

    def forward(layer_rows, first_gain, query_mat, key_mat, value_mat, out_mat, second_gain, router_mat, gate_mat, up_mat, down_mat):
        seq_rows = layer_rows.reshape(-1, SEQ, D)
        seq_segs = segments.reshape(-1, SEQ)

        def per_sequence(inputs):
            return attention_layer(inputs[0], inputs[1], first_gain, query_mat, key_mat, value_mat, out_mat)
        middle = lax.map(jax.checkpoint(per_sequence), (seq_rows, seq_segs)).reshape(-1, D)

        def per_block(inputs):
            return expert_layer(inputs[0], inputs[1], second_gain, router_mat, gate_mat, up_mat, down_mat)
        result = lax.map(jax.checkpoint(per_block), (middle.reshape(-1, token_rows, D), routes.reshape(-1, token_rows, TOPK)))
        return result.reshape(-1, D)
    floats = tuple((array.astype(jnp.float32) for array in (layer_input, norm1_gain, w_query, w_key, w_value, w_output, norm2_gain, router, w_gate, w_up, w_down)))
    layer_out, pullback = jax.vjp(forward, *floats)
    grads = pullback(cotangent.astype(jnp.float32))
    return (layer_out.astype(jnp.bfloat16), grads[0], grads[1], grads[2], grads[3], grads[4], grads[5], grads[6], grads[7], grads[8], grads[9], grads[10])
```

```python
import functools

import jax
import jax.numpy as jnp
import numpy as np
from jax import lax
from jax.experimental import pallas as pl
from jax.experimental.pallas import tpu as pltpu
from jax.sharding import PartitionSpec as P

HD = 64
WINDOW = 1024
SEQ = 2048
QB = 256
EPS = 1e-05
NEG = -1e30
MIB = 1 << 20
f32 = jnp.float32
bf16 = jnp.bfloat16
i32 = jnp.int32

NT = (((1,), (1,)), ((), ()))
TN = (((0,), (0,)), ((), ()))
NN = (((1,), (0,)), ((), ()))


def mm(a, b, dims=NN):
    return lax.dot_general(a, b, dims, preferred_element_type=f32)


def params(mib, n=1):
    return pltpu.CompilerParams(
        vmem_limit_bytes=mib * MIB, dimension_semantics=("arbitrary",) * n
    )


def cost(gflop, mb):
    return pl.CostEstimate(
        flops=int(gflop * 1e9), bytes_accessed=int(mb * 1e6), transcendentals=0
    )


def rope_tables():
    half = HD // 2
    freq = (10000.0 ** (-np.arange(half, dtype=np.float32) / half)).astype(np.float32)
    angles = (np.arange(SEQ, dtype=np.float32)[:, None] * freq[None, :]).astype(np.float32)
    cos, sin = np.cos(angles), np.sin(angles)
    return (
        np.concatenate([cos] * 4, axis=1).astype(np.float32),
        np.concatenate([-sin, sin] * 2, axis=1).astype(np.float32),
    )


def swap_halves(u):
    lane = lax.broadcasted_iota(i32, u.shape, 1) % HD
    return jnp.where(lane < HD // 2, pltpu.roll(u, 2 * HD - HD // 2, 1), pltpu.roll(u, HD // 2, 1))


def qkv_kernel(x_ref, gain_ref, wq_ref, wk_ref, wv_ref, cos_ref, sin_ref,
               n_ref, q_ref, k_ref, v_ref, kt_ref):
    x = x_ref[...].astype(f32)
    inv = lax.rsqrt(jnp.mean(x * x, axis=-1, keepdims=True) + EPS)
    normed = (x * inv * gain_ref[...].astype(f32)).astype(bf16)
    n_ref[...] = normed
    cos, sin = cos_ref[...], sin_ref[...]
    q = mm(normed, wq_ref[...])
    for c in range(q.shape[1] // 128):
        u = q[:, 128 * c:128 * (c + 1)]
        r = ((u * cos + swap_halves(u) * sin) * HD ** (-0.5)).astype(bf16)
        q_ref[2 * c] = r[:, :HD]
        q_ref[2 * c + 1] = r[:, HD:]
    k = mm(normed, wk_ref[...])
    v = mm(normed, wv_ref[...])
    for c in range(k.shape[1] // 128):
        u = k[:, 128 * c:128 * (c + 1)]
        r = u * cos + swap_halves(u) * sin
        rb = r.astype(bf16)
        k_ref[2 * c] = rb[:, :HD]
        k_ref[2 * c + 1] = rb[:, HD:]
        rt = jnp.transpose(r).astype(bf16)
        kt_ref[2 * c] = rt[:HD]
        kt_ref[2 * c + 1] = rt[HD:]
        vb = v[:, 128 * c:128 * (c + 1)].astype(bf16)
        v_ref[2 * c] = vb[:, :HD]
        v_ref[2 * c + 1] = vb[:, HD:]


def qkv_call(x, gain, wq, wk, wv, cos, sin):
    rows, width = x.shape
    rb = 512
    qc, kc = wq.shape[1], wk.shape[1]
    qh, kh = qc // HD, kc // HD
    per_seq = SEQ // rb
    whole = lambda shape: pl.BlockSpec(shape, lambda i: (0,) * len(shape))
    return pl.pallas_call(
        qkv_kernel,
        grid=(rows // rb,),
        in_specs=[
            pl.BlockSpec((rb, width), lambda i: (i, 0)),
            whole((1, width)), whole((width, qc)), whole((width, kc)), whole((width, kc)),
            pl.BlockSpec((rb, 128), lambda i: (i % per_seq, 0)),
            pl.BlockSpec((rb, 128), lambda i: (i % per_seq, 0)),
        ],
        out_specs=[
            pl.BlockSpec((rb, width), lambda i: (i, 0)),
            pl.BlockSpec((qh, rb, HD), lambda i: (0, i, 0)),
            pl.BlockSpec((kh, rb, HD), lambda i: (0, i, 0)),
            pl.BlockSpec((kh, rb, HD), lambda i: (0, i, 0)),
            pl.BlockSpec((kh, HD, rb), lambda i: (0, 0, i)),
        ],
        out_shape=[
            jax.ShapeDtypeStruct((rows, width), bf16),
            jax.ShapeDtypeStruct((qh, rows, HD), bf16),
            jax.ShapeDtypeStruct((kh, rows, HD), bf16),
            jax.ShapeDtypeStruct((kh, rows, HD), bf16),
            jax.ShapeDtypeStruct((kh, HD, rows), bf16),
        ],
        compiler_params=params(48),
        cost_estimate=cost(13, 20),
        name="norm_qkv",
    )(x, gain, wq, wk, wv, cos, sin)


def window_blocks():
    return WINDOW // QB + 1


def on_block(i, body):
    most = window_blocks()
    for j in range(most - 1):
        pl.when(i == j)(functools.partial(body, j + 1, 0))
    pl.when(i >= most - 1)(
        lambda: body(most, pl.multiple_of((i - (most - 1)) * QB, QB))
    )


def attend_kernel(order_ref, q_ref, k_ref, v_ref, segq_ref, segk_ref, wo_ref, *rest):
    heads_ref, lse_ref, send_ref, keep_ref, bias_ref = rest[-5:]
    step = pl.program_id(0)
    i = order_ref[step]
    qh, kh = q_ref.shape[0], k_ref.shape[0]
    group = qh // kh

    def body(blocks, start):
        span = blocks * QB
        segq = segq_ref[...]
        segq = jnp.where(segq == 0, -1, segq)
        row = lax.broadcasted_iota(i32, (QB, QB), 0)
        col = lax.broadcasted_iota(i32, (QB, QB), 1)
        for j in range(blocks):
            same = segk_ref[:, pl.ds(start + j * QB, QB)] == segq
            if j == blocks - 1:
                same = (same & (col <= row)) | (col == row)
            elif blocks == window_blocks() and j == 0:
                same = same & (row < col)
            bias_ref[:, j * QB:(j + 1) * QB] = jnp.where(same, 0.0, NEG)
        lane = lax.broadcasted_iota(i32, (QB, 128), 1)
        logs = jnp.zeros((QB, 128), f32)
        outs = []
        for g in range(kh):
            q = q_ref[g * group:(g + 1) * group].reshape(group * QB, HD)
            k = k_ref[g, pl.ds(start, span), :]
            v = v_ref[g, pl.ds(start, span), :]
            s = mm(q, k, NT).reshape(group, QB, span) + bias_ref[:, :span][None]
            top = jnp.max(s, axis=-1, keepdims=True)
            p = jnp.exp(s - top)
            total = jnp.sum(p, axis=-1, keepdims=True)
            o = mm(p.astype(bf16).reshape(group * QB, span), v).reshape(group, QB, HD)
            o = (o * (1.0 / total)).astype(bf16)
            log = top + jnp.log(total)
            for h in range(group):
                outs.append(o[h])
                logs = jnp.where(lane == g * group + h, log[h], logs)
        heads = jnp.concatenate(outs, axis=1)
        heads_ref[...] = heads
        lse_ref[...] = jnp.transpose(logs)[:lse_ref.shape[0]]
        part = mm(heads, wo_ref[...]).astype(bf16)

        @pl.when(step < 2)
        def _():
            send_ref[...] = part

        @pl.when(step >= 2)
        def _():
            keep_ref[...] = part

    on_block(i, body)


def attend_call(order, q, k, v, seg_col, seg_row, wo, held=None):
    qh, rows, _ = q.shape
    kh = k.shape[0]
    width = wo.shape[1]
    lse_rows = -(-qh // 8) * 8
    in_specs = [
        pl.BlockSpec((qh, QB, HD), lambda s, o: (0, o[s], 0)),
        pl.BlockSpec((kh, rows, HD), lambda s, o: (0, 0, 0)),
        pl.BlockSpec((kh, rows, HD), lambda s, o: (0, 0, 0)),
        pl.BlockSpec((QB, 1), lambda s, o: (o[s], 0)),
        pl.BlockSpec((1, rows), lambda s, o: (0, 0)),
        pl.BlockSpec((qh * HD, width), lambda s, o: (0, 0)),
    ]
    args = [q, k, v, seg_col, seg_row, wo]
    aliases = {}
    if held is not None:
        aliases = {1 + len(args): 0, 2 + len(args): 1}
        args += list(held)
        in_specs += [pl.BlockSpec(memory_space=pl.ANY)] * 2
    return pl.pallas_call(
        attend_kernel,
        grid_spec=pltpu.PrefetchScalarGridSpec(
            num_scalar_prefetch=1,
            grid=(4,),
            in_specs=in_specs,
            out_specs=[
                pl.BlockSpec((QB, qh * HD), lambda s, o: (o[s], 0)),
                pl.BlockSpec((lse_rows, QB), lambda s, o: (0, o[s])),
                pl.BlockSpec((QB, width), lambda s, o: (jnp.minimum(s, 1), 0)),
                pl.BlockSpec((QB, width), lambda s, o: (jnp.maximum(s - 2, 0), 0)),
            ],
            scratch_shapes=[pltpu.VMEM((QB, window_blocks() * QB), f32)],
        ),
        out_shape=[
            jax.ShapeDtypeStruct((rows, qh * HD), bf16),
            jax.ShapeDtypeStruct((lse_rows, rows), f32),
            jax.ShapeDtypeStruct((2 * QB, width), bf16),
            jax.ShapeDtypeStruct((2 * QB, width), bf16),
        ],
        input_output_aliases=aliases,
        compiler_params=params(56),
        cost_estimate=cost(17, 10),
        name="attend",
    )(order, *args)


def attend_back_kernel(last, order_ref, q_ref, k_ref, v_ref, kt_ref, segq_ref, segk_ref,
                       heads_ref, lse_ref, dba_ref, dbb_ref, wo_ref, cos_ref, sin_ref, *rest):
    if last:
        (cosk_ref, sink_ref, dk_in, dv_in, _, dq_ref, dkv_ref,
         bias_ref, dk_ref, dv_ref, p_ref, ds_ref) = rest
    else:
        dq_ref, dk_ref, dv_ref, bias_ref, p_ref, ds_ref = rest
    step = pl.program_id(0)
    i = order_ref[step]
    qh, kh = q_ref.shape[0], k_ref.shape[0]
    group = qh // kh

    @pl.when(step == 0)
    def _():
        dk_ref[...] = dk_in[...] if last else jnp.zeros_like(dk_ref)
        dv_ref[...] = dv_in[...] if last else jnp.zeros_like(dv_ref)

    def body(blocks, start):
        span = blocks * QB
        segq = segq_ref[...]
        segq = jnp.where(segq == 0, -1, segq)
        row = lax.broadcasted_iota(i32, (QB, QB), 1)
        col = lax.broadcasted_iota(i32, (QB, QB), 0)
        for j in range(blocks):
            same = segk_ref[pl.ds(start + j * QB, QB), :] == segq
            if j == blocks - 1:
                same = (same & (col <= row)) | (col == row)
            elif blocks == window_blocks() and j == 0:
                same = same & (row < col)
            bias_ref[j * QB:(j + 1) * QB, :] = jnp.where(same, 0.0, NEG)
        db = jnp.where(step < 2, dba_ref[...], dbb_ref[...])
        heads = heads_ref[...]
        dh = mm(db, wo_ref[...], NT).astype(bf16)
        prod = jnp.transpose(dh.astype(f32) * heads.astype(f32))
        dqs = []
        for g in range(kh):
            k = k_ref[g, pl.ds(start, span), :]
            v = v_ref[g, pl.ds(start, span), :]
            dos = []
            for h in range(group):
                at = g * group + h
                do = dh[:, at * HD:(at + 1) * HD]
                dos.append(do)
                delta = jnp.sum(prod[at * HD:(at + 1) * HD], axis=0, keepdims=True)
                s = mm(k, q_ref[at], NT) + bias_ref[:span]
                p = jnp.exp(s - lse_ref[at:at + 1, :])
                dp = mm(v, do, NT)
                p_ref[:span, h * QB:(h + 1) * QB] = p.astype(bf16)
                ds_ref[:span, h * QB:(h + 1) * QB] = (p * (dp - delta)).astype(bf16)
            q = q_ref[g * group:(g + 1) * group].reshape(group * QB, HD)
            dk_ref[g, pl.ds(start, span), :] += mm(ds_ref[:span], q)
            dv_ref[g, pl.ds(start, span), :] += mm(p_ref[:span], jnp.concatenate(dos, axis=0))
            dq = mm(kt_ref[g, :, pl.ds(start, span)], ds_ref[:span]) * HD ** (-0.5)
            for h in range(group):
                dqs.append(dq[:, h * QB:(h + 1) * QB])
        dq = jnp.transpose(jnp.concatenate(dqs, axis=0))
        cos, sin = cos_ref[...], sin_ref[...]
        for c in range(dq.shape[1] // 128):
            u = dq[:, 128 * c:128 * (c + 1)]
            dq_ref[:, 128 * c:128 * (c + 1)] = (u * cos - swap_halves(u) * sin).astype(bf16)

    on_block(i, body)

    if last:
        @pl.when(step == pl.num_programs(0) - 1)
        def _():
            for c in range(kh // 2):
                u = jnp.concatenate([dk_ref[2 * c], dk_ref[2 * c + 1]], axis=1)
                u = u * cosk_ref[...] - swap_halves(u) * sink_ref[...]
                dkv_ref[:, 128 * c:128 * (c + 1)] = u.astype(bf16)
                w = jnp.concatenate([dv_ref[2 * c], dv_ref[2 * c + 1]], axis=1)
                dkv_ref[:, (kh // 2 + c) * 128:(kh // 2 + c + 1) * 128] = w.astype(bf16)


def attend_back_call(order, q, k, v, kt, seg_row, seg_col, heads, lse, db_a, db_b, wo, cos, sin,
                     held=None):
    qh, rows, _ = q.shape
    kh = k.shape[0]
    width = wo.shape[1]
    span = window_blocks() * QB
    group = qh // kh
    last = held is not None
    whole = lambda shape: pl.BlockSpec(shape, lambda s, o: (0,) * len(shape))
    in_specs = [
        pl.BlockSpec((qh, QB, HD), lambda s, o: (0, o[s], 0)),
        whole((kh, rows, HD)), whole((kh, rows, HD)), whole((kh, HD, rows)),
        pl.BlockSpec((1, QB), lambda s, o: (0, o[s])),
        whole((rows, 1)),
        pl.BlockSpec((QB, qh * HD), lambda s, o: (o[s], 0)),
        pl.BlockSpec((lse.shape[0], QB), lambda s, o: (0, o[s])),
        pl.BlockSpec((QB, width), lambda s, o: (jnp.minimum(s, 1), 0)),
        pl.BlockSpec((QB, width), lambda s, o: (jnp.maximum(s - 2, 0), 0)),
        whole((qh * HD, width)),
        pl.BlockSpec((QB, 128), lambda s, o: (o[s], 0)),
        pl.BlockSpec((QB, 128), lambda s, o: (o[s], 0)),
    ]
    args = [q, k, v, kt, seg_row, seg_col, heads, lse, db_a, db_b, wo, cos, sin]
    out_specs = [pl.BlockSpec((QB, qh * HD), lambda s, o: (o[s], 0))]
    out_shape = [jax.ShapeDtypeStruct((rows, qh * HD), bf16)]
    scratch = [pltpu.VMEM((span, QB), f32)]
    aliases = {}
    if last:
        dq, dk, dv = held
        aliases = {1 + len(args) + 4: 0}
        args += [cos, sin, dk, dv, dq]
        in_specs += [whole((rows, 128)), whole((rows, 128)), whole((kh, rows, HD)),
                     whole((kh, rows, HD)), pl.BlockSpec(memory_space=pl.ANY)]
        out_specs += [whole((rows, 2 * kh * HD))]
        out_shape += [jax.ShapeDtypeStruct((rows, 2 * kh * HD), bf16)]
        scratch += [pltpu.VMEM((kh, rows, HD), f32)] * 2
    else:
        out_specs += [whole((kh, rows, HD))] * 2
        out_shape += [jax.ShapeDtypeStruct((kh, rows, HD), f32)] * 2
    scratch += [pltpu.VMEM((span, group * QB), bf16)] * 2
    return pl.pallas_call(
        functools.partial(attend_back_kernel, last),
        grid_spec=pltpu.PrefetchScalarGridSpec(
            num_scalar_prefetch=1, grid=(4,),
            in_specs=in_specs, out_specs=out_specs, scratch_shapes=scratch,
        ),
        out_shape=out_shape,
        input_output_aliases=aliases,
        compiler_params=params(58),
        cost_estimate=cost(22, 20),
        name="attend_back",
    )(order, *args)


def qkv_back_kernel(order_ref, dq_ref, dkv_ref, x_ref, wq_ref, wk_ref, wv_ref,
                    send_ref, keep_ref, gain_ref):
    step = pl.program_id(0)
    half = pl.num_programs(0) // 2
    kc = wk_ref.shape[1]
    total = (
        mm(dq_ref[...], wq_ref[...], NT)
        + mm(dkv_ref[:, :kc], wk_ref[...], NT)
        + mm(dkv_ref[:, kc:], wv_ref[...], NT)
    )

    @pl.when(step < half)
    def _():
        send_ref[...] = total.astype(bf16)

    @pl.when(step >= half)
    def _():
        keep_ref[...] = total.astype(bf16)

    x = x_ref[...].astype(f32)
    inv = lax.rsqrt(jnp.mean(x * x, axis=-1, keepdims=True) + EPS)
    gain = jnp.sum(total * (x * inv), axis=0, keepdims=True)
    gain_ref[...] = jnp.where(step == 0, gain, gain_ref[...] + gain)


def qkv_back_call(order, dq, dkv, x, wq, wk, wv):
    rows, width = x.shape
    steps = order.shape[0]
    rb = rows // steps
    half = steps // 2
    whole = lambda shape: pl.BlockSpec(shape, lambda s, o: (0,) * len(shape))
    return pl.pallas_call(
        qkv_back_kernel,
        grid_spec=pltpu.PrefetchScalarGridSpec(
            num_scalar_prefetch=1, grid=(steps,),
            in_specs=[
                pl.BlockSpec((rb, dq.shape[1]), lambda s, o: (o[s], 0)),
                pl.BlockSpec((rb, dkv.shape[1]), lambda s, o: (o[s], 0)),
                pl.BlockSpec((rb, width), lambda s, o: (o[s], 0)),
                whole(wq.shape), whole(wk.shape), whole(wv.shape),
            ],
            out_specs=[
                pl.BlockSpec((rb, width), lambda s, o: (jnp.minimum(s, half - 1), 0)),
                pl.BlockSpec((rb, width), lambda s, o: (jnp.maximum(s - half, 0), 0)),
                whole((1, width)),
            ],
        ),
        out_shape=[
            jax.ShapeDtypeStruct((rows // 2, width), bf16),
            jax.ShapeDtypeStruct((rows // 2, width), bf16),
            jax.ShapeDtypeStruct((1, width), f32),
        ],
        compiler_params=params(48),
        cost_estimate=cost(6, 20),
        name="qkv_back",
    )(order, dq, dkv, x, wq, wk, wv)


def expert_kernel(sources, cap, experts, base_ref, *refs):
    x_refs, refs = refs[:2 * sources], refs[2 * sources:]
    c_refs, refs = refs[:sources], refs[sources:]
    router_ref, wg_ref, wu_ref, wd_ref = refs[:4]
    refs = refs[-(4 * sources + 6 + 4):]
    out_refs, refs = refs[:2 * sources], refs[2 * sources:]
    back_refs, refs = refs[:2 * sources], refs[2 * sources:]
    (dmix_ref, xs_ref, cs_ref, act_ref, dg_ref, du_ref,
     mix_ref, rank_ref, so_ref, sd_ref) = refs
    e = pl.program_id(0)
    local = pl.num_programs(0)
    half = x_refs[0].shape[0]
    quarter = 2 * half
    extra = c_refs[0].shape[0] - quarter
    slots = so_ref.shape[1]
    base = base_ref[0]

    @pl.when(e == 0)
    def _():
        for s in range(sources):
            tail = c_refs[s][quarter:, :].astype(f32)
            rank = jnp.concatenate(
                [tail[:, j * quarter:(j + 1) * quarter] for j in range(-(-experts // extra))],
                axis=0,
            )[:experts].astype(i32)
            rank_ref[s] = rank
            logits = jnp.concatenate(
                [mm(router_ref[...], x_refs[2 * s + j][...], NT) for j in range(2)], axis=1
            )
            chosen = rank >= 0
            logits = jnp.where(chosen, logits, NEG)
            top = jnp.max(logits, axis=0, keepdims=True)
            ex = jnp.where(chosen, jnp.exp(logits - top), 0.0)
            mix_ref[s] = ex / jnp.sum(ex, axis=0, keepdims=True)

    slot_row = lax.broadcasted_iota(i32, (cap, quarter), 0)
    picks, mixes = [], []
    for s in range(sources):
        hot = slot_row == rank_ref[s, pl.ds(base + e, 1), :]
        pick = jnp.where(hot, 1.0, 0.0)
        picks.append(pick)
        mixes.append(jnp.sum(pick * mix_ref[s, pl.ds(base + e, 1), :], axis=1, keepdims=True))
        pick = pick.astype(bf16)
        xs_ref[0, s * cap:(s + 1) * cap, :] = (
            mm(pick[:, :half], x_refs[2 * s][...]) + mm(pick[:, half:], x_refs[2 * s + 1][...])
        ).astype(bf16)
        cs_ref[0, s * cap:(s + 1) * cap, :] = mm(pick, c_refs[s][:quarter, :]).astype(bf16)
    mix = jnp.concatenate(mixes, axis=0)
    xs, cs = xs_ref[0], cs_ref[0]
    gate, up = mm(xs, wg_ref[0]), mm(xs, wu_ref[0])
    d_act = mm(cs, wd_ref[0], NT)
    sig = jax.nn.sigmoid(gate)
    silu = gate * sig
    act = silu * up
    d_mix = jnp.sum(act * d_act, axis=1, keepdims=True)
    for s in range(sources):
        dmix_ref[s, pl.ds(e, 1), :] = jnp.sum(
            picks[s] * d_mix[s * cap:(s + 1) * cap], axis=0, keepdims=True
        )
    d_act = d_act * mix
    act = (act * mix).astype(bf16)
    du = (d_act * silu).astype(bf16)
    dg = (d_act * up * sig * (1.0 + gate * (1.0 - sig))).astype(bf16)
    act_ref[0], du_ref[0], dg_ref[0] = act, du, dg
    so = mm(act, wd_ref[0]).astype(bf16)
    sd = (mm(dg, wg_ref[0], NT) + mm(du, wu_ref[0], NT)).astype(bf16)
    at = pl.multiple_of(e * cap, 16)
    for s in range(sources):
        so_ref[s, pl.ds(at, cap), :] = so[s * cap:(s + 1) * cap]
        sd_ref[s, pl.ds(at, cap), :] = sd[s * cap:(s + 1) * cap]

    @pl.when(e == local - 1)
    def _():
        count = slots // cap
        col = lax.broadcasted_iota(i32, (quarter, slots), 1)
        for s in range(sources):
            rows = [rank_ref[s, pl.ds(base + j, 1), :] for j in range(count)]
            rows = [jnp.where(r >= 0, r + j * cap, -1) for j, r in enumerate(rows)]
            rows += [jnp.full((1, quarter), -1, i32)] * (-count % 8)
            back = jnp.transpose(jnp.concatenate(rows, axis=0))
            hot = None
            for j in range(count):
                this = back[:, j:j + 1] == col
                hot = this if hot is None else hot | this
            pick = jnp.where(hot, 1.0, 0.0).astype(bf16)
            for j in range(2):
                part = pick[j * half:(j + 1) * half]
                out_refs[2 * s + j][...] = mm(part, so_ref[s]).astype(bf16)
                back_refs[2 * s + j][...] = mm(part, sd_ref[s]).astype(bf16)


def expert_call(base, xs, cs, router_t, wg, wu, wd, cap, at, of, held=None):
    sources = len(cs)
    experts = router_t.shape[0]
    local, width, hidden = wg.shape
    half = xs[0][0].shape[0]
    quarter = 2 * half
    xs = [part for halves in xs for part in halves]
    sizes = (width, width, hidden, hidden, hidden)
    whole = lambda shape: pl.BlockSpec(shape, lambda e, b: (0,) * len(shape))
    slot_spec = lambda n: pl.BlockSpec((1, sources * cap, n), lambda e, b: (e, at, 0))
    args = [*xs, *cs, router_t, wg, wu, wd]
    in_specs = (
        [whole(a.shape) for a in (*xs, *cs, router_t)]
        + [
            pl.BlockSpec((1, width, hidden), lambda e, b: (e, 0, 0)),
            pl.BlockSpec((1, width, hidden), lambda e, b: (e, 0, 0)),
            pl.BlockSpec((1, hidden, width), lambda e, b: (e, 0, 0)),
        ]
    )
    aliases = {}
    if held is not None:
        aliases = {1 + len(args) + j: 4 * sources + 1 + j for j in range(5)}
        args += list(held)
        in_specs += [pl.BlockSpec(memory_space=pl.ANY)] * 5
    outs = pl.pallas_call(
        functools.partial(expert_kernel, sources, cap, experts),
        grid_spec=pltpu.PrefetchScalarGridSpec(
            num_scalar_prefetch=1,
            grid=(local,),
            in_specs=in_specs,
            out_specs=[whole((half, width))] * (4 * sources)
            + [whole((sources, local, quarter))]
            + [slot_spec(n) for n in sizes],
            scratch_shapes=[
                pltpu.VMEM((sources, experts, quarter), f32),
                pltpu.VMEM((sources, experts, quarter), i32),
                pltpu.VMEM((sources, local * cap, width), bf16),
                pltpu.VMEM((sources, local * cap, width), bf16),
            ],
        ),
        out_shape=[jax.ShapeDtypeStruct((half, width), bf16)] * (4 * sources)
        + [jax.ShapeDtypeStruct((sources, local, quarter), f32)]
        + [jax.ShapeDtypeStruct((local, of * cap, n), bf16) for n in sizes],
        input_output_aliases=aliases,
        compiler_params=params(60),
        cost_estimate=cost(14 * sources, 20),
        name="experts",
    )(base, *args)
    halves = lambda a: [(a[2 * s], a[2 * s + 1]) for s in range(sources)]
    return (
        halves(outs[:2 * sources]),
        halves(outs[2 * sources:4 * sources]),
        outs[4 * sources],
        outs[4 * sources + 1:],
    )


def weight_grad_kernel(order_ref, a_ref, b_ref, send_ref, keep_ref):
    part = mm(a_ref[0], b_ref[0], TN).astype(bf16)
    step = pl.program_id(0)

    @pl.when(step < 2)
    def _():
        send_ref[0, 0] = part

    @pl.when(step >= 2)
    def _():
        keep_ref[0, 0] = part


def weight_grad_call(order, a, b):
    local, slots, width = a.shape
    hidden = b.shape[2]
    cut = width // 4
    shape = jax.ShapeDtypeStruct((2, local, cut, hidden), bf16)
    return pl.pallas_call(
        weight_grad_kernel,
        grid_spec=pltpu.PrefetchScalarGridSpec(
            num_scalar_prefetch=1,
            grid=(4, local),
            in_specs=[
                pl.BlockSpec((1, slots, cut), lambda s, e, o: (e, 0, o[s])),
                pl.BlockSpec((1, slots, hidden), lambda s, e, o: (e, 0, 0)),
            ],
            out_specs=[
                pl.BlockSpec(
                    (1, 1, cut, hidden),
                    lambda s, e, o: (jnp.minimum(s, 1), jnp.where(s < 2, e, local - 1), 0, 0),
                ),
                pl.BlockSpec(
                    (1, 1, cut, hidden),
                    lambda s, e, o: (jnp.maximum(s - 2, 0), jnp.where(s < 2, 0, e), 0, 0),
                ),
            ],
        ),
        out_shape=[shape, shape],
        compiler_params=params(40, 2),
        cost_estimate=cost(10, 20),
        name="weight_grad",
    )(order, a, b)


def ring_of(n):
    return list(range(0, n, 2)) + list(range(n - 1, 0, -2))


def ring_moves(n):
    ring = ring_of(n)
    ahead = [(ring[p], ring[(p + 1) % n]) for p in range(n)]
    return ahead, [(b, a) for a, b in ahead]


def add_low(a, b):
    return (a.astype(f32) + b.astype(f32)).astype(bf16)


def ring_gather(own, n, split):
    ahead, behind = ring_moves(n)
    if split:
        cut = own.shape[0] // 2
        own = (own[:cut], own[cut:])
    else:
        cut = own.shape[0] // 32 * 16
        own = (own,)
    a = b = own
    got = []
    for _ in range(n // 2 - 1):
        a = tuple(lax.ppermute(v, "dp", ahead) for v in a)
        b = tuple(lax.ppermute(v, "dp", behind) for v in b)
        got.append([a, b] if split else [a[0], b[0]])
    if split:
        got.append([(lax.ppermute(a[0], "dp", ahead), lax.ppermute(b[1], "dp", behind))])
    else:
        a, b = lax.ppermute(a[0][:cut], "dp", ahead), lax.ppermute(b[0][cut:], "dp", behind)
        got.append([jnp.concatenate([a, b], axis=0)])
    return own, got


def ring_scatter(own, parts, n, between=()):
    ahead, behind = ring_moves(n)
    far = parts[-1][0]
    a, b = [far[0], None], [None, far[1]]
    came, done = [], []
    for step in range(n // 2):
        if step > 0:
            minus, plus = parts[n // 2 - step - 1]
            sums = [add_low(v, t) for v, t in zip(a + b, plus + minus) if v is not None]
            if step <= len(between):
                done.append(between[step - 1](came[step - 2] if step > 1 else None))
                sums = after(done[-1], sums)
            sums = iter(sums)
            a = [t if v is None else next(sums) for v, t in zip(a, plus)]
            b = [t if v is None else next(sums) for v, t in zip(b, minus)]
        a = [None if v is None else lax.ppermute(v, "dp", ahead) for v in a]
        b = [None if v is None else lax.ppermute(v, "dp", behind) for v in b]
        came.append([v for v in a + b if v is not None])
    return [o.astype(f32) + x.astype(f32) + y.astype(f32) for o, x, y in zip(own, a, b)], done


CORE = [(0, 1), (1, 0), (2, 3), (3, 2)]
CHIP = [(0, 2), (2, 0), (1, 3), (3, 1)]


def to_core(a):
    return lax.ppermute(a, "tensor", CORE)


def to_chip(a):
    return lax.ppermute(a, "tensor", CHIP)


def after(first, then):
    return lax.optimization_barrier((then, first))[0]


def per_device(layer_input, segments, routes, norm1_gain, w_query, w_key, w_value, w_output,
               norm2_gain, router, w_gate, w_up, w_down, cotangent, n_dp):
    tokens_dev, width = layer_input.shape
    quarter, top_count = routes.shape
    experts = router.shape[1]
    local = w_gate.shape[0]
    cap = quarter * top_count * 5 // (4 * experts)
    hidden = w_gate.shape[2]
    t_rank = lax.axis_index("tensor")
    d_rank = lax.axis_index("dp")
    place = jnp.where(d_rank % 2 == 0, d_rank // 2, n_dp - 1 - d_rank // 2)
    ringed = n_dp <= 8
    cos, sin = rope_tables()

    hot_t = jnp.any(
        routes.T[:, None, :] == jnp.arange(experts, dtype=i32)[None, :, None], axis=0
    )
    before = (jnp.arange(quarter)[:, None] < jnp.arange(quarter)[None, :]).astype(bf16)
    rank_t = jnp.dot(hot_t.astype(bf16), before, preferred_element_type=f32)
    rank_t = jnp.where(hot_t, rank_t, -1.0).astype(bf16)
    per_row = width // quarter
    extra = 16 * -(-experts // (16 * per_row))
    rank_rows = jnp.concatenate(
        [rank_t, jnp.full((extra * per_row - experts, quarter), -1.0, bf16)], axis=0
    ).reshape(per_row, extra, quarter)
    rank_rows = jnp.concatenate([rank_rows[j] for j in range(per_row)], axis=1)
    payload = jnp.concatenate([cotangent, rank_rows], axis=0)
    router_t = router.T
    ahead, behind = ring_moves(n_dp)

    normed1, q, k, v, kt = qkv_call(
        layer_input, norm1_gain[None, :], w_query, w_key, w_value, cos, sin
    )
    if ringed:
        _, grads_from = ring_gather(payload, n_dp, False)
        stage = [after(g, jnp.zeros((), i32)) for g in grads_from]
    else:
        stage = [jnp.zeros((), i32)] * 2
    seg_col, seg_row = segments[:, None], segments[None, :]
    pair = lambda t: jnp.stack([2 * t, 2 * t + 1])
    mate, other, cross = t_rank ^ 1, t_rank ^ 2, t_rank ^ 3
    quarters = jnp.stack([cross, mate, other, t_rank]).astype(i32)
    first = jnp.concatenate([pair(cross), pair(other)]).astype(i32)
    second = jnp.concatenate([pair(mate), pair(t_rank)]).astype(i32)
    heads, lse, send_a, keep_a = attend_call(first, q, k, v, seg_col, seg_row, w_output)
    far = to_chip(add_low(keep_a, to_core(send_a)))
    heads, lse, send_b, keep_b = attend_call(
        second + stage[0], q, k, v, seg_col, seg_row, w_output, held=(heads, lse)
    )
    far = far + stage[1].astype(bf16)
    branch = keep_b.astype(f32) + to_core(send_b).astype(f32) + far.astype(f32)

    row_start = t_rank * quarter
    own_input = lax.dynamic_slice_in_dim(layer_input, row_start, quarter).astype(f32)
    middle = own_input + branch
    inv_rms2 = lax.rsqrt(jnp.mean(middle * middle, axis=-1, keepdims=True) + EPS)
    gain_two = norm2_gain.astype(f32)
    normed2 = (middle * inv_rms2 * gain_two).astype(bf16)

    base = (d_rank * local).astype(i32)[None]
    run = lambda xs, cs, at, of, held: expert_call(
        base, xs, cs, router_t, w_gate, w_up, w_down, cap, at, of, held
    )
    if ringed:
        own, rows_from = ring_gather(normed2, n_dp, True)
        (out_own,), (back_own,), dmix_own, held = run([own], [payload], n_dp - 1, n_dp, None)
        outs, backs, dmix_minus, dmix_plus = [], [], [], []
        for j, (xs, cs) in enumerate(zip(rows_from, grads_from)):
            at = j if len(xs) == 2 else n_dp - 2
            o, b, m, held = run(xs, cs, at, n_dp, held)
            outs.append(o)
            backs.append(b)
            dmix_minus.append(m[0])
            dmix_plus.append(m[-1])
        by_step = jnp.stack([dmix_own[0]] + dmix_plus + dmix_minus[-2::-1])
        where = jnp.asarray(
            [d // 2 if d % 2 == 0 else n_dp - 1 - d // 2 for d in range(n_dp)], i32
        )
        dmix_part = jnp.take(by_step, (where - place) % n_dp, axis=0)
        grad_of = lambda i, j: lambda came: weight_grad_call(
            quarters if came is None else quarters + after(came, jnp.zeros((), i32)),
            held[i], held[j],
        )
        routed, expert_parts = ring_scatter(
            back_own, backs, n_dp, (grad_of(0, 3), grad_of(0, 4), grad_of(1, 2))
        )
        routed = jnp.concatenate(routed, axis=0)
    else:
        grads_all = lax.all_gather(payload, "dp", axis=0)
        rows_all = lax.all_gather(normed2, "dp", axis=0)
        halves = lambda a: (a[:quarter // 2], a[quarter // 2:])

        def two(sums, pair_rows):
            x, c = pair_rows
            o, b, m, held = run([halves(x[0]), halves(x[1])], [c[0], c[1]], 0, 2, None)
            grads = [
                list(weight_grad_call(quarters, held[i], held[j])) for i, j in ((0, 3), (0, 4), (1, 2))
            ]
            sums = jax.tree.map(lambda t, g: t + g.astype(f32), sums, grads)
            join = lambda a: jnp.stack([jnp.concatenate(h, axis=0) for h in a])
            return sums, (join(o), join(b), m)

        pairs = lambda a: a.reshape((n_dp // 2, 2) + a.shape[1:])
        zero = jnp.zeros((2, local, width // 4, hidden), f32)
        expert_parts, (outs, backs, dmix_part) = lax.scan(
            two, [[zero, zero]] * 3, (pairs(rows_all), pairs(grads_all))
        )
        expert_parts = jax.tree.map(lambda a: a.astype(bf16), expert_parts)
        dmix_part = dmix_part.reshape(n_dp, local, quarter)
        scatter = lambda a: lax.psum_scatter(
            a.reshape(n_dp * quarter, width), "dp", scatter_dimension=0, tiled=True
        ).astype(f32)
        routed = scatter(backs)
    d_mix = lax.all_to_all(dmix_part, "dp", split_axis=0, concat_axis=0, tiled=True)
    d_mix = d_mix.reshape(experts, quarter)

    logits_t = mm(router_t, normed2, NT)
    logits_t = jnp.where(hot_t, logits_t, -jnp.inf)
    mix_t = jax.nn.softmax(logits_t, axis=0)
    d_logits_t = mix_t * (d_mix - jnp.sum(mix_t * d_mix, axis=0, keepdims=True))
    d_logits = jnp.where(hot_t, d_logits_t, 0.0).astype(bf16).T
    router_part = mm(normed2, d_logits, TN)

    out_grad = cotangent.astype(f32)
    d_normed2 = routed + mm(d_logits, router, NT)
    scaled_two = d_normed2 * gain_two
    d_middle = (
        out_grad
        + inv_rms2 * scaled_two
        - middle * inv_rms2**3 * jnp.mean(scaled_two * middle, axis=-1, keepdims=True)
    )

    db_own = d_middle.astype(bf16)
    db_mate = to_core(db_own)
    db_other = to_chip(db_own)
    db_cross = to_core(db_other)
    near = jnp.concatenate([pair(t_rank), pair(mate)]).astype(i32)
    distant = jnp.concatenate([pair(other), pair(cross)]).astype(i32)
    common = (q, k, v, kt, seg_row, seg_col, heads, lse)
    dq, dk, dv = attend_back_call(near, *common, db_own, db_mate, w_output, cos, sin)
    rows_of = lambda t: lax.dynamic_slice_in_dim(heads, t * quarter, quarter)
    wo_near = mm(db_own, rows_of(t_rank), TN) + mm(db_mate, rows_of(mate), TN)
    dq, dkv = attend_back_call(
        distant, *common, db_other, db_cross, w_output, cos, sin, held=(dq, dk, dv)
    )
    send, keep, first_gain_part = qkv_back_call(
        jnp.concatenate([pair(t) for t in (cross, mate, other, t_rank)]).astype(i32),
        dq, dkv, layer_input, w_query, w_key, w_value,
    )
    came = to_core(send)
    far = to_chip(add_low(keep[:quarter], came[:quarter]))
    d_normed1 = keep[quarter:].astype(f32) + came[quarter:].astype(f32) + far.astype(f32)

    second_gain_part = jnp.sum(d_normed2 * middle * inv_rms2, axis=0)

    def over_all(part):
        rows = part.reshape(n_dp * 4, -1)
        rows = lax.all_to_all(rows, ("dp", "tensor"), split_axis=0, concat_axis=0, tiled=True)
        return jnp.sum(rows, axis=0)

    router_gain = jnp.concatenate([router_part, second_gain_part[:, None]], axis=1)
    router_gain = over_all(router_gain).reshape(-1, experts + 1)
    first_gain = over_all(first_gain_part)

    if ringed:
        summed, _ = ring_scatter(out_own, [list(after(db_own, o)) for o in outs], n_dp)
        summed = jnp.concatenate(summed, axis=0)
    else:
        summed = scatter(outs)
    layer_out = (middle + summed).astype(bf16)

    def shared(parts):
        send, keep = parts
        came = to_core(send)
        far = to_chip(add_low(keep[0], came[0]))
        return keep[1].astype(f32) + came[1].astype(f32) + far.astype(f32)

    gate_grad, up_grad, down_grad = [shared(p) for p in expert_parts]
    down_grad = jnp.transpose(down_grad, (0, 2, 1))

    query_part = mm(normed1, dq, TN).astype(bf16)
    kv_part = mm(normed1, dkv, TN).astype(bf16)
    wo_part = wo_near + mm(db_other, rows_of(other), TN) + mm(db_cross, rows_of(cross), TN)
    packed_dense = jnp.concatenate([query_part, kv_part, wo_part.astype(bf16)], axis=1)
    if ringed:
        blocks = packed_dense.reshape(n_dp, width // n_dp, packed_dense.shape[1])
        ring = jnp.asarray(ring_of(n_dp), i32)

        def block(far):
            rows = lax.dynamic_index_in_dim(
                blocks, ring[(place + far) % n_dp], axis=0, keepdims=False
            )
            return rows[:rows.shape[0] // 2], rows[rows.shape[0] // 2:]

        parts = [[block(-j), block(j)] for j in range(1, n_dp // 2)] + [[block(n_dp // 2)]]
        dense_sum, _ = ring_scatter(block(0), parts, n_dp)
        dense_sum = jnp.concatenate(dense_sum, axis=0)
    else:
        dense_sum = lax.psum_scatter(
            packed_dense, "dp", scatter_dimension=0, tiled=True
        ).astype(f32)
    q_cols, kv_cols = w_query.shape[1], w_key.shape[1]
    query_grad = dense_sum[:, :q_cols]
    key_grad = dense_sum[:, q_cols:q_cols + kv_cols]
    value_grad = dense_sum[:, q_cols + kv_cols:q_cols + 2 * kv_cols]
    output_grad = jnp.transpose(dense_sum[:, q_cols + 2 * kv_cols:])

    own_rms = lax.rsqrt(jnp.mean(own_input * own_input, axis=-1, keepdims=True) + EPS)
    scaled_one = d_normed1 * norm1_gain.astype(f32)
    input_grad = (
        d_middle
        + own_rms * scaled_one
        - own_input * own_rms**3 * jnp.mean(scaled_one * own_input, axis=-1, keepdims=True)
    )
    return (
        layer_out,
        input_grad,
        first_gain,
        query_grad,
        key_grad,
        value_grad,
        output_grad,
        router_gain[:, experts],
        router_gain[:, :experts],
        gate_grad,
        up_grad,
        down_grad,
    )


def solution(mesh):
    both = ("dp", "tensor")
    return jax.shard_map(
        functools.partial(per_device, n_dp=mesh.shape["dp"]),
        mesh=mesh,
        in_specs=(
            P("dp", None), P("dp"), P(both, None), P(),
            P(None, "tensor"), P(None, "tensor"), P(None, "tensor"), P("tensor", None),
            P(), P(), P("dp", None, None), P("dp", None, None), P("dp", None, None),
            P(both, None),
        ),
        out_specs=(
            P(both, None), P(both, None), P(both), P("dp", "tensor"), P("dp", "tensor"),
            P("dp", "tensor"), P("tensor", "dp"), P(both), P(both, None),
            P("dp", "tensor", None), P("dp", "tensor", None), P("dp", None, "tensor"),
        ),
        check_vma=False,
    )
```

```python
import functools

import jax
import jax.numpy as jnp
import numpy as np
from jax import lax
from jax.experimental import pallas as pl
from jax.experimental.pallas import tpu as pltpu
from jax.sharding import PartitionSpec as P

HD = 64
WINDOW = 1024
SEQ = 2048
QB = 256
EPS = 1e-05
NEG = -1e30
MIB = 1 << 20
f32 = jnp.float32
bf16 = jnp.bfloat16
i32 = jnp.int32

NT = (((1,), (1,)), ((), ()))
TN = (((0,), (0,)), ((), ()))
NN = (((1,), (0,)), ((), ()))


def mm(a, b, dims=NN):
    return lax.dot_general(a, b, dims, preferred_element_type=f32)


def params(mib, n=1):
    return pltpu.CompilerParams(
        vmem_limit_bytes=mib * MIB, dimension_semantics=("arbitrary",) * n
    )


WEIGHT = 1.0


def takes(us):
    return pl.CostEstimate(
        flops=int(us * WEIGHT * 1.153e9), bytes_accessed=1_000_000, transcendentals=0
    )


def rope_tables():
    half = HD // 2
    freq = (10000.0 ** (-np.arange(half, dtype=np.float32) / half)).astype(np.float32)
    angles = (np.arange(SEQ, dtype=np.float32)[:, None] * freq[None, :]).astype(np.float32)
    cos, sin = np.cos(angles), np.sin(angles)
    return (
        np.concatenate([cos] * 4, axis=1).astype(np.float32),
        np.concatenate([-sin, sin] * 2, axis=1).astype(np.float32),
    )


def swap_halves(u):
    lane = lax.broadcasted_iota(i32, u.shape, 1) % HD
    return jnp.where(lane < HD // 2, pltpu.roll(u, 2 * HD - HD // 2, 1), pltpu.roll(u, HD // 2, 1))


def qkv_kernel(x_ref, gain_ref, wq_ref, wk_ref, wv_ref, cos_ref, sin_ref,
               n_ref, q_ref, k_ref, v_ref, kt_ref):
    x = x_ref[...].astype(f32)
    inv = lax.rsqrt(jnp.mean(x * x, axis=-1, keepdims=True) + EPS)
    normed = (x * inv * gain_ref[...].astype(f32)).astype(bf16)
    n_ref[...] = normed
    cos, sin = cos_ref[...], sin_ref[...]
    q = mm(normed, wq_ref[...])
    for c in range(q.shape[1] // 128):
        u = q[:, 128 * c:128 * (c + 1)]
        r = ((u * cos + swap_halves(u) * sin) * HD ** (-0.5)).astype(bf16)
        q_ref[2 * c] = r[:, :HD]
        q_ref[2 * c + 1] = r[:, HD:]
    k = mm(normed, wk_ref[...])
    v = mm(normed, wv_ref[...])
    for c in range(k.shape[1] // 128):
        u = k[:, 128 * c:128 * (c + 1)]
        r = u * cos + swap_halves(u) * sin
        rb = r.astype(bf16)
        k_ref[2 * c] = rb[:, :HD]
        k_ref[2 * c + 1] = rb[:, HD:]
        rt = jnp.transpose(r).astype(bf16)
        kt_ref[2 * c] = rt[:HD]
        kt_ref[2 * c + 1] = rt[HD:]
        vb = v[:, 128 * c:128 * (c + 1)].astype(bf16)
        v_ref[2 * c] = vb[:, :HD]
        v_ref[2 * c + 1] = vb[:, HD:]


def qkv_call(x, gain, wq, wk, wv, cos, sin):
    rows, width = x.shape
    rb = 512
    qc, kc = wq.shape[1], wk.shape[1]
    qh, kh = qc // HD, kc // HD
    per_seq = SEQ // rb
    whole = lambda shape: pl.BlockSpec(shape, lambda i: (0,) * len(shape))
    return pl.pallas_call(
        qkv_kernel,
        grid=(rows // rb,),
        in_specs=[
            pl.BlockSpec((rb, width), lambda i: (i, 0)),
            whole((1, width)), whole((width, qc)), whole((width, kc)), whole((width, kc)),
            pl.BlockSpec((rb, 128), lambda i: (i % per_seq, 0)),
            pl.BlockSpec((rb, 128), lambda i: (i % per_seq, 0)),
        ],
        out_specs=[
            pl.BlockSpec((rb, width), lambda i: (i, 0)),
            pl.BlockSpec((qh, rb, HD), lambda i: (0, i, 0)),
            pl.BlockSpec((kh, rb, HD), lambda i: (0, i, 0)),
            pl.BlockSpec((kh, rb, HD), lambda i: (0, i, 0)),
            pl.BlockSpec((kh, HD, rb), lambda i: (0, 0, i)),
        ],
        out_shape=[
            jax.ShapeDtypeStruct((rows, width), bf16),
            jax.ShapeDtypeStruct((qh, rows, HD), bf16),
            jax.ShapeDtypeStruct((kh, rows, HD), bf16),
            jax.ShapeDtypeStruct((kh, rows, HD), bf16),
            jax.ShapeDtypeStruct((kh, HD, rows), bf16),
        ],
        compiler_params=params(48),
        cost_estimate=takes(99),
        name="norm_qkv",
    )(x, gain, wq, wk, wv, cos, sin)


def window_blocks():
    return WINDOW // QB + 1


def on_block(i, body):
    most = window_blocks()
    for j in range(most - 1):
        pl.when(i == j)(functools.partial(body, j + 1, 0))
    pl.when(i >= most - 1)(
        lambda: body(most, pl.multiple_of((i - (most - 1)) * QB, QB))
    )


def attend_kernel(order_ref, q_ref, k_ref, v_ref, segq_ref, segk_ref, wo_ref, *rest):
    heads_ref, lse_ref, send_ref, keep_ref, bias_ref = rest[-5:]
    step = pl.program_id(0)
    i = order_ref[step]
    qh, kh = q_ref.shape[0], k_ref.shape[0]
    group = qh // kh

    def body(blocks, start):
        span = blocks * QB
        segq = segq_ref[...]
        segq = jnp.where(segq == 0, -1, segq)
        row = lax.broadcasted_iota(i32, (QB, QB), 0)
        col = lax.broadcasted_iota(i32, (QB, QB), 1)
        for j in range(blocks):
            same = segk_ref[:, pl.ds(start + j * QB, QB)] == segq
            if j == blocks - 1:
                same = (same & (col <= row)) | (col == row)
            elif blocks == window_blocks() and j == 0:
                same = same & (row < col)
            bias_ref[:, j * QB:(j + 1) * QB] = jnp.where(same, 0.0, NEG)
        lane = lax.broadcasted_iota(i32, (QB, 128), 1)
        logs = jnp.zeros((QB, 128), f32)
        outs = []
        for g in range(kh):
            q = q_ref[g * group:(g + 1) * group].reshape(group * QB, HD)
            k = k_ref[g, pl.ds(start, span), :]
            v = v_ref[g, pl.ds(start, span), :]
            s = mm(q, k, NT).reshape(group, QB, span) + bias_ref[:, :span][None]
            top = jnp.max(s, axis=-1, keepdims=True)
            p = jnp.exp(s - top)
            total = jnp.sum(p, axis=-1, keepdims=True)
            o = mm(p.astype(bf16).reshape(group * QB, span), v).reshape(group, QB, HD)
            o = (o * (1.0 / total)).astype(bf16)
            log = top + jnp.log(total)
            for h in range(group):
                outs.append(o[h])
                logs = jnp.where(lane == g * group + h, log[h], logs)
        heads = jnp.concatenate(outs, axis=1)
        heads_ref[...] = heads
        lse_ref[...] = jnp.transpose(logs)[:lse_ref.shape[0]]
        part = mm(heads, wo_ref[...]).astype(bf16)

        @pl.when(step < 2)
        def _():
            send_ref[...] = part

        @pl.when(step >= 2)
        def _():
            keep_ref[...] = part

    on_block(i, body)


def attend_call(order, q, k, v, seg_col, seg_row, wo, held=None):
    qh, rows, _ = q.shape
    kh = k.shape[0]
    width = wo.shape[1]
    lse_rows = -(-qh // 8) * 8
    in_specs = [
        pl.BlockSpec((qh, QB, HD), lambda s, o: (0, o[s], 0)),
        pl.BlockSpec((kh, rows, HD), lambda s, o: (0, 0, 0)),
        pl.BlockSpec((kh, rows, HD), lambda s, o: (0, 0, 0)),
        pl.BlockSpec((QB, 1), lambda s, o: (o[s], 0)),
        pl.BlockSpec((1, rows), lambda s, o: (0, 0)),
        pl.BlockSpec((qh * HD, width), lambda s, o: (0, 0)),
    ]
    args = [q, k, v, seg_col, seg_row, wo]
    aliases = {}
    if held is not None:
        aliases = {1 + len(args): 0, 2 + len(args): 1}
        args += list(held)
        in_specs += [pl.BlockSpec(memory_space=pl.ANY)] * 2
    return pl.pallas_call(
        attend_kernel,
        grid_spec=pltpu.PrefetchScalarGridSpec(
            num_scalar_prefetch=1,
            grid=(4,),
            in_specs=in_specs,
            out_specs=[
                pl.BlockSpec((QB, qh * HD), lambda s, o: (o[s], 0)),
                pl.BlockSpec((lse_rows, QB), lambda s, o: (0, o[s])),
                pl.BlockSpec((QB, width), lambda s, o: (jnp.minimum(s, 1), 0)),
                pl.BlockSpec((QB, width), lambda s, o: (jnp.maximum(s - 2, 0), 0)),
            ],
            scratch_shapes=[pltpu.VMEM((QB, window_blocks() * QB), f32)],
        ),
        out_shape=[
            jax.ShapeDtypeStruct((rows, qh * HD), bf16),
            jax.ShapeDtypeStruct((lse_rows, rows), f32),
            jax.ShapeDtypeStruct((2 * QB, width), bf16),
            jax.ShapeDtypeStruct((2 * QB, width), bf16),
        ],
        input_output_aliases=aliases,
        compiler_params=params(56),
        cost_estimate=takes(1),
        name="attend",
    )(order, *args)


def attend_back_kernel(last, order_ref, q_ref, k_ref, v_ref, kt_ref, segq_ref, segk_ref,
                       heads_ref, lse_ref, dba_ref, dbb_ref, wo_ref, cos_ref, sin_ref, *rest):
    if last:
        (cosk_ref, sink_ref, dk_in, dv_in, _, dq_ref, dkv_ref,
         bias_ref, dk_ref, dv_ref, p_ref, ds_ref) = rest
    else:
        dq_ref, dk_ref, dv_ref, bias_ref, p_ref, ds_ref = rest
    step = pl.program_id(0)
    i = order_ref[step]
    qh, kh = q_ref.shape[0], k_ref.shape[0]
    group = qh // kh

    @pl.when(step == 0)
    def _():
        dk_ref[...] = dk_in[...] if last else jnp.zeros_like(dk_ref)
        dv_ref[...] = dv_in[...] if last else jnp.zeros_like(dv_ref)

    def body(blocks, start):
        span = blocks * QB
        segq = segq_ref[...]
        segq = jnp.where(segq == 0, -1, segq)
        row = lax.broadcasted_iota(i32, (QB, QB), 1)
        col = lax.broadcasted_iota(i32, (QB, QB), 0)
        for j in range(blocks):
            same = segk_ref[pl.ds(start + j * QB, QB), :] == segq
            if j == blocks - 1:
                same = (same & (col <= row)) | (col == row)
            elif blocks == window_blocks() and j == 0:
                same = same & (row < col)
            bias_ref[j * QB:(j + 1) * QB, :] = jnp.where(same, 0.0, NEG)
        db = jnp.where(step < 2, dba_ref[...], dbb_ref[...])
        heads = heads_ref[...]
        dh = mm(db, wo_ref[...], NT).astype(bf16)
        prod = jnp.transpose(dh.astype(f32) * heads.astype(f32))
        dqs = []
        for g in range(kh):
            k = k_ref[g, pl.ds(start, span), :]
            v = v_ref[g, pl.ds(start, span), :]
            dos = []
            for h in range(group):
                at = g * group + h
                do = dh[:, at * HD:(at + 1) * HD]
                dos.append(do)
                delta = jnp.sum(prod[at * HD:(at + 1) * HD], axis=0, keepdims=True)
                s = mm(k, q_ref[at], NT) + bias_ref[:span]
                p = jnp.exp(s - lse_ref[at:at + 1, :])
                dp = mm(v, do, NT)
                p_ref[:span, h * QB:(h + 1) * QB] = p.astype(bf16)
                ds_ref[:span, h * QB:(h + 1) * QB] = (p * (dp - delta)).astype(bf16)
            q = q_ref[g * group:(g + 1) * group].reshape(group * QB, HD)
            dk_ref[g, pl.ds(start, span), :] += mm(ds_ref[:span], q)
            dv_ref[g, pl.ds(start, span), :] += mm(p_ref[:span], jnp.concatenate(dos, axis=0))
            dq = mm(kt_ref[g, :, pl.ds(start, span)], ds_ref[:span]) * HD ** (-0.5)
            for h in range(group):
                dqs.append(dq[:, h * QB:(h + 1) * QB])
        dq = jnp.transpose(jnp.concatenate(dqs, axis=0))
        cos, sin = cos_ref[...], sin_ref[...]
        for c in range(dq.shape[1] // 128):
            u = dq[:, 128 * c:128 * (c + 1)]
            dq_ref[:, 128 * c:128 * (c + 1)] = (u * cos - swap_halves(u) * sin).astype(bf16)

    on_block(i, body)

    if last:
        @pl.when(step == pl.num_programs(0) - 1)
        def _():
            for c in range(kh // 2):
                u = jnp.concatenate([dk_ref[2 * c], dk_ref[2 * c + 1]], axis=1)
                u = u * cosk_ref[...] - swap_halves(u) * sink_ref[...]
                dkv_ref[:, 128 * c:128 * (c + 1)] = u.astype(bf16)
                w = jnp.concatenate([dv_ref[2 * c], dv_ref[2 * c + 1]], axis=1)
                dkv_ref[:, (kh // 2 + c) * 128:(kh // 2 + c + 1) * 128] = w.astype(bf16)


def attend_back_call(order, q, k, v, kt, seg_row, seg_col, heads, lse, db_a, db_b, wo, cos, sin,
                     held=None):
    qh, rows, _ = q.shape
    kh = k.shape[0]
    width = wo.shape[1]
    span = window_blocks() * QB
    group = qh // kh
    last = held is not None
    whole = lambda shape: pl.BlockSpec(shape, lambda s, o: (0,) * len(shape))
    in_specs = [
        pl.BlockSpec((qh, QB, HD), lambda s, o: (0, o[s], 0)),
        whole((kh, rows, HD)), whole((kh, rows, HD)), whole((kh, HD, rows)),
        pl.BlockSpec((1, QB), lambda s, o: (0, o[s])),
        whole((rows, 1)),
        pl.BlockSpec((QB, qh * HD), lambda s, o: (o[s], 0)),
        pl.BlockSpec((lse.shape[0], QB), lambda s, o: (0, o[s])),
        pl.BlockSpec((QB, width), lambda s, o: (jnp.minimum(s, 1), 0)),
        pl.BlockSpec((QB, width), lambda s, o: (jnp.maximum(s - 2, 0), 0)),
        whole((qh * HD, width)),
        pl.BlockSpec((QB, 128), lambda s, o: (o[s], 0)),
        pl.BlockSpec((QB, 128), lambda s, o: (o[s], 0)),
    ]
    args = [q, k, v, kt, seg_row, seg_col, heads, lse, db_a, db_b, wo, cos, sin]
    out_specs = [pl.BlockSpec((QB, qh * HD), lambda s, o: (o[s], 0))]
    out_shape = [jax.ShapeDtypeStruct((rows, qh * HD), bf16)]
    scratch = [pltpu.VMEM((span, QB), f32)]
    aliases = {}
    if last:
        dq, dk, dv = held
        aliases = {1 + len(args) + 4: 0}
        args += [cos, sin, dk, dv, dq]
        in_specs += [whole((rows, 128)), whole((rows, 128)), whole((kh, rows, HD)),
                     whole((kh, rows, HD)), pl.BlockSpec(memory_space=pl.ANY)]
        out_specs += [whole((rows, 2 * kh * HD))]
        out_shape += [jax.ShapeDtypeStruct((rows, 2 * kh * HD), bf16)]
        scratch += [pltpu.VMEM((kh, rows, HD), f32)] * 2
    else:
        out_specs += [whole((kh, rows, HD))] * 2
        out_shape += [jax.ShapeDtypeStruct((kh, rows, HD), f32)] * 2
    scratch += [pltpu.VMEM((span, group * QB), bf16)] * 2
    return pl.pallas_call(
        functools.partial(attend_back_kernel, last),
        grid_spec=pltpu.PrefetchScalarGridSpec(
            num_scalar_prefetch=1, grid=(4,),
            in_specs=in_specs, out_specs=out_specs, scratch_shapes=scratch,
        ),
        out_shape=out_shape,
        input_output_aliases=aliases,
        compiler_params=params(34),
        cost_estimate=takes(27),
        name="attend_back",
    )(order, *args)


def qkv_back_kernel(order_ref, dq_ref, dkv_ref, wq_ref, wk_ref, wv_ref, send_ref, keep_ref):
    step = pl.program_id(0)
    half = pl.num_programs(0) // 2
    kc = wk_ref.shape[1]
    total = (
        mm(dq_ref[...], wq_ref[...], NT)
        + mm(dkv_ref[:, :kc], wk_ref[...], NT)
        + mm(dkv_ref[:, kc:], wv_ref[...], NT)
    ).astype(bf16)

    @pl.when(step < half)
    def _():
        send_ref[...] = total

    @pl.when(step >= half)
    def _():
        keep_ref[...] = total


def qkv_back_call(order, dq, dkv, wq, wk, wv):
    rows, width = dq.shape[0], wq.shape[0]
    steps = order.shape[0]
    rb = rows // steps
    half = steps // 2
    whole = lambda shape: pl.BlockSpec(shape, lambda s, o: (0,) * len(shape))
    return pl.pallas_call(
        qkv_back_kernel,
        grid_spec=pltpu.PrefetchScalarGridSpec(
            num_scalar_prefetch=1, grid=(steps,),
            in_specs=[
                pl.BlockSpec((rb, dq.shape[1]), lambda s, o: (o[s], 0)),
                pl.BlockSpec((rb, dkv.shape[1]), lambda s, o: (o[s], 0)),
                whole(wq.shape), whole(wk.shape), whole(wv.shape),
            ],
            out_specs=[
                pl.BlockSpec((rb, width), lambda s, o: (jnp.minimum(s, half - 1), 0)),
                pl.BlockSpec((rb, width), lambda s, o: (jnp.maximum(s - half, 0), 0)),
            ],
        ),
        out_shape=[jax.ShapeDtypeStruct((rows // 2, width), bf16)] * 2,
        compiler_params=params(20),
        cost_estimate=takes(9),
        name="qkv_back",
    )(order, dq, dkv, wq, wk, wv)


def dense_grad_kernel(order_ref, n_ref, dq_ref, dkv_ref, db0_ref, db1_ref, db2_ref, db3_ref,
                      heads_ref, first_ref, second_ref, dlog_ref, gain2_ref, gain_ref,
                      wq_ref, wk_ref, wv_ref, out_ref):
    qc, kvc = dq_ref.shape[1], dkv_ref.shape[1]
    quarter = db0_ref.shape[0]
    normed = n_ref[...]
    query, key_value = mm(normed, dq_ref[...], TN), mm(normed, dkv_ref[...], TN)
    out_ref[:, :qc] = query.astype(bf16)
    out_ref[:, qc:qc + kvc] = key_value.astype(bf16)
    first = (
        jnp.sum(query * wq_ref[...].astype(f32), axis=1, keepdims=True)
        + jnp.sum(key_value[:, :kvc // 2] * wk_ref[...].astype(f32), axis=1, keepdims=True)
        + jnp.sum(key_value[:, kvc // 2:] * wv_ref[...].astype(f32), axis=1, keepdims=True)
    )
    wo = None
    for j, db_ref in enumerate((db0_ref, db1_ref, db2_ref, db3_ref)):
        at = pl.multiple_of(order_ref[j] * quarter, quarter)
        part = mm(db_ref[...], heads_ref[pl.ds(at, quarter), :], TN)
        wo = part if wo is None else wo + part
    out_ref[:, qc + kvc:2 * qc + kvc] = wo.astype(bf16)
    half = first_ref.shape[0]
    router = (
        mm(first_ref[...], dlog_ref[:half, :], TN) + mm(second_ref[...], dlog_ref[half:, :], TN)
    )
    cols = router.shape[0]
    column = lambda row: jnp.transpose(jnp.broadcast_to(row.astype(f32), (8, cols)))[:, :1]
    pad = out_ref.shape[1] - (2 * qc + kvc) - router.shape[1] - 2
    out_ref[:, 2 * qc + kvc:] = jnp.concatenate(
        [router, column(gain2_ref[...]), first / column(gain_ref[...]), jnp.zeros((cols, pad), f32)],
        axis=1,
    ).astype(bf16)


def dense_grad_call(order, normed1, dq, dkv, dbs, heads, normed2, d_logits, gain2, gain, ws):
    rows, width = normed1.shape
    qc, kvc = dq.shape[1], dkv.shape[1]
    cols = width // 6
    lanes = 2 * qc + kvc + -(-(d_logits.shape[1] + 2) // 128) * 128
    whole = lambda a: pl.BlockSpec(a.shape, lambda s, o: (0, 0))
    block = lambda a: pl.BlockSpec((a.shape[0], cols), lambda s, o: (0, s))
    lines = lambda a: pl.BlockSpec((cols, a.shape[1]), lambda s, o: (s, 0))
    return pl.pallas_call(
        dense_grad_kernel,
        grid_spec=pltpu.PrefetchScalarGridSpec(
            num_scalar_prefetch=1,
            grid=(6,),
            in_specs=[block(normed1), whole(dq), whole(dkv), *map(block, dbs), whole(heads),
                      *map(block, normed2), whole(d_logits), block(gain2), block(gain),
                      *map(lines, ws)],
            out_specs=pl.BlockSpec((cols, lanes), lambda s, o: (s, 0)),
        ),
        out_shape=jax.ShapeDtypeStruct((width, lanes), bf16),
        compiler_params=params(36),
        cost_estimate=takes(13),
        name="dense_grad",
    )(order, normed1, dq, dkv, *dbs, heads, *normed2, d_logits, gain2, gain, *ws)


def expert_kernel(sources, cap, experts, base_ref, *refs):
    x_refs, refs = refs[:2 * sources], refs[2 * sources:]
    c_refs, refs = refs[:sources], refs[sources:]
    router_ref, wg_ref, wu_ref, wd_ref = refs[:4]
    refs = refs[-(4 * sources + 5 + 5):]
    out_refs, refs = refs[:2 * sources], refs[2 * sources:]
    back_refs, refs = refs[:2 * sources], refs[2 * sources:]
    (xs_ref, cs_ref, act_ref, dg_ref, du_ref,
     mix_ref, rank_ref, dmix_ref, so_ref, sd_ref) = refs
    e = pl.program_id(0)
    local = pl.num_programs(0)
    half = x_refs[0].shape[0]
    quarter = 2 * half
    extra = c_refs[0].shape[0] - quarter
    slots = so_ref.shape[1]
    base = base_ref[0]

    @pl.when(e == 0)
    def _():
        for s in range(sources):
            tail = c_refs[s][quarter:, :].astype(f32)
            rank = jnp.concatenate(
                [tail[:, j * quarter:(j + 1) * quarter] for j in range(-(-experts // extra))],
                axis=0,
            )[:experts].astype(i32)
            rank_ref[s] = rank
            logits = jnp.concatenate(
                [mm(router_ref[...], x_refs[2 * s + j][...], NT) for j in range(2)], axis=1
            )
            chosen = rank >= 0
            logits = jnp.where(chosen, logits, NEG)
            top = jnp.max(logits, axis=0, keepdims=True)
            ex = jnp.where(chosen, jnp.exp(logits - top), 0.0)
            mix_ref[s] = ex / jnp.sum(ex, axis=0, keepdims=True)

    slot_row = lax.broadcasted_iota(i32, (cap, quarter), 0)
    picks, mixes = [], []
    for s in range(sources):
        hot = slot_row == rank_ref[s, pl.ds(base + e, 1), :]
        pick = jnp.where(hot, 1.0, 0.0)
        picks.append(pick)
        mixes.append(jnp.sum(pick * mix_ref[s, pl.ds(base + e, 1), :], axis=1, keepdims=True))
        pick = pick.astype(bf16)
        xs_ref[0, s * cap:(s + 1) * cap, :] = (
            mm(pick[:, :half], x_refs[2 * s][...]) + mm(pick[:, half:], x_refs[2 * s + 1][...])
        ).astype(bf16)
        cs_ref[0, s * cap:(s + 1) * cap, :] = mm(pick, c_refs[s][:quarter, :]).astype(bf16)
    mix = jnp.concatenate(mixes, axis=0)
    xs, cs = xs_ref[0], cs_ref[0]
    gate, up = mm(xs, wg_ref[0]), mm(xs, wu_ref[0])
    d_act = mm(cs, wd_ref[0], NT)
    sig = jax.nn.sigmoid(gate)
    silu = gate * sig
    act = silu * up
    d_mix = jnp.sum(act * d_act, axis=1, keepdims=True)
    for s in range(sources):
        dmix_ref[s, pl.ds(e, 1), :] = jnp.sum(
            picks[s] * d_mix[s * cap:(s + 1) * cap], axis=0, keepdims=True
        )
    d_act = d_act * mix
    act = (act * mix).astype(bf16)
    du = (d_act * silu).astype(bf16)
    dg = (d_act * up * sig * (1.0 + gate * (1.0 - sig))).astype(bf16)
    act_ref[0], du_ref[0], dg_ref[0] = act, du, dg
    so = mm(act, wd_ref[0]).astype(bf16)
    sd = (mm(dg, wg_ref[0], NT) + mm(du, wu_ref[0], NT)).astype(bf16)
    at = pl.multiple_of(e * cap, 16)
    for s in range(sources):
        so_ref[s, pl.ds(at, cap), :] = so[s * cap:(s + 1) * cap]
        sd_ref[s, pl.ds(at, cap), :] = sd[s * cap:(s + 1) * cap]

    @pl.when(e == local - 1)
    def _():
        count = slots // cap
        col = lax.broadcasted_iota(i32, (quarter, slots), 1)
        for s in range(sources):
            rows = [rank_ref[s, pl.ds(base + j, 1), :] for j in range(count)]
            rows = [jnp.where(r >= 0, r + j * cap, -1) for j, r in enumerate(rows)]
            rows += [jnp.full((1, quarter), -1, i32)] * (-count % 8)
            back = jnp.transpose(jnp.concatenate(rows, axis=0))
            hot = None
            for j in range(count):
                this = back[:, j:j + 1] == col
                hot = this if hot is None else hot | this
            pick = jnp.where(hot, 1.0, 0.0).astype(bf16)
            for j in range(2):
                part = pick[j * half:(j + 1) * half]
                out_refs[2 * s + j][...] = mm(part, so_ref[s]).astype(bf16)
                back_refs[2 * s + j][:half, :] = mm(part, sd_ref[s]).astype(bf16)
            row = lax.broadcasted_iota(i32, (extra, quarter), 0)
            sums = [jnp.zeros((extra, quarter), f32) for _ in range(x_refs[0].shape[1] // quarter)]
            for j in range(count):
                line = dmix_ref[s, j:j + 1, :]
                for piece in range(len(sums)):
                    sums[piece] = jnp.where(row + piece * extra == base + j, line, sums[piece])
            sums = jnp.concatenate(sums, axis=1)
            high = sums.astype(bf16)
            back_refs[2 * s + 1][half:half + extra, :] = high
            back_refs[2 * s + 1][half + extra:, :] = (sums - high.astype(f32)).astype(bf16)


def expert_call(base, xs, cs, router_t, wg, wu, wd, cap, at, of, held=None):
    sources = len(cs)
    experts = router_t.shape[0]
    local, width, hidden = wg.shape
    half = xs[0][0].shape[0]
    quarter = 2 * half
    xs = [part for halves in xs for part in halves]
    rows = [half] * (2 * sources) + [half, half + 2 * (cs[0].shape[0] - quarter)] * sources
    sizes = (width, width, hidden, hidden, hidden)
    whole = lambda shape: pl.BlockSpec(shape, lambda e, b: (0,) * len(shape))
    slot_spec = lambda n: pl.BlockSpec((1, sources * cap, n), lambda e, b: (e, at, 0))
    args = [*xs, *cs, router_t, wg, wu, wd]
    in_specs = (
        [whole(a.shape) for a in (*xs, *cs, router_t)]
        + [
            pl.BlockSpec((1, width, hidden), lambda e, b: (e, 0, 0)),
            pl.BlockSpec((1, width, hidden), lambda e, b: (e, 0, 0)),
            pl.BlockSpec((1, hidden, width), lambda e, b: (e, 0, 0)),
        ]
    )
    aliases = {}
    if held is not None:
        aliases = {1 + len(args) + j: 4 * sources + j for j in range(5)}
        args += list(held)
        in_specs += [pl.BlockSpec(memory_space=pl.ANY)] * 5
    outs = pl.pallas_call(
        functools.partial(expert_kernel, sources, cap, experts),
        grid_spec=pltpu.PrefetchScalarGridSpec(
            num_scalar_prefetch=1,
            grid=(local,),
            in_specs=in_specs,
            out_specs=[whole((n, width)) for n in rows] + [slot_spec(n) for n in sizes],
            scratch_shapes=[
                pltpu.VMEM((sources, experts, quarter), f32),
                pltpu.VMEM((sources, experts, quarter), i32),
                pltpu.VMEM((sources, local, quarter), f32),
                pltpu.VMEM((sources, local * cap, width), bf16),
                pltpu.VMEM((sources, local * cap, width), bf16),
            ],
        ),
        out_shape=[jax.ShapeDtypeStruct((n, width), bf16) for n in rows]
        + [jax.ShapeDtypeStruct((local, of * cap, n), bf16) for n in sizes],
        input_output_aliases=aliases,
        compiler_params=params(60),
        cost_estimate=takes(12 + 11 * sources),
        name="experts",
    )(base, *args)
    halves = lambda a: [(a[2 * s], a[2 * s + 1]) for s in range(sources)]
    return (
        halves(outs[:2 * sources]),
        halves(outs[2 * sources:4 * sources]),
        outs[4 * sources:],
    )


def weight_grad_kernel(order_ref, a_ref, b_ref, send_ref, keep_ref):
    part = mm(a_ref[0], b_ref[0], TN).astype(bf16)
    step = pl.program_id(0)

    @pl.when(step < 2)
    def _():
        send_ref[0, 0] = part

    @pl.when(step >= 2)
    def _():
        keep_ref[0, 0] = part


def weight_grad_call(order, a, b, cut_last=False):
    local, slots, width = (b if cut_last else a).shape
    cut = width // 4
    part = lambda x: pl.BlockSpec((1, slots, cut), lambda s, e, o: (e, 0, o[s]))
    full = lambda x: pl.BlockSpec((1, slots, x.shape[2]), lambda s, e, o: (e, 0, 0))
    dims = (a.shape[2], cut) if cut_last else (cut, b.shape[2])
    shape = jax.ShapeDtypeStruct((2, local, *dims), bf16)
    return pl.pallas_call(
        weight_grad_kernel,
        grid_spec=pltpu.PrefetchScalarGridSpec(
            num_scalar_prefetch=1,
            grid=(4, local),
            in_specs=[full(a), part(b)] if cut_last else [part(a), full(b)],
            out_specs=[
                pl.BlockSpec(
                    (1, 1, *dims),
                    lambda s, e, o: (jnp.minimum(s, 1), jnp.where(s < 2, e, local - 1), 0, 0),
                ),
                pl.BlockSpec(
                    (1, 1, *dims),
                    lambda s, e, o: (jnp.maximum(s - 2, 0), jnp.where(s < 2, 0, e), 0, 0),
                ),
            ],
        ),
        out_shape=[shape, shape],
        compiler_params=params(20, 2),
        cost_estimate=takes(18),
        name="weight_grad",
    )(order, a, b)


def norm_two_kernel(at_ref, x_ref, keep_ref, came_ref, far_ref, gain_ref,
                    middle_ref, first_ref, second_ref):
    step = pl.program_id(0)
    branch = keep_ref[...].astype(f32) + came_ref[...].astype(f32) + far_ref[...].astype(f32)
    middle = x_ref[...].astype(f32) + branch
    middle_ref[...] = middle
    inv = lax.rsqrt(jnp.mean(middle * middle, axis=-1, keepdims=True) + EPS)
    normed = (middle * inv * gain_ref[...].astype(f32)).astype(bf16)

    @pl.when(step < pl.num_programs(0) // 2)
    def _():
        first_ref[...] = normed

    @pl.when(step >= pl.num_programs(0) // 2)
    def _():
        second_ref[...] = normed


def norm_two_call(t_rank, x, keep, came, far, gain):
    quarter, width = keep.shape
    rb = quarter // 4
    row = pl.BlockSpec((rb, width), lambda s, t: (s, 0))
    return pl.pallas_call(
        norm_two_kernel,
        grid_spec=pltpu.PrefetchScalarGridSpec(
            num_scalar_prefetch=1,
            grid=(4,),
            in_specs=[
                pl.BlockSpec((rb, width), lambda s, t: (4 * t[0] + s, 0)), row, row, row,
                pl.BlockSpec((1, width), lambda s, t: (0, 0)),
            ],
            out_specs=[
                row,
                pl.BlockSpec((rb, width), lambda s, t: (jnp.minimum(s, 1), 0)),
                pl.BlockSpec((rb, width), lambda s, t: (jnp.maximum(s - 2, 0), 0)),
            ],
        ),
        out_shape=[
            jax.ShapeDtypeStruct((quarter, width), f32),
            jax.ShapeDtypeStruct((quarter // 2, width), bf16),
            jax.ShapeDtypeStruct((quarter // 2, width), bf16),
        ],
        compiler_params=params(12),
        cost_estimate=takes(3),
        name="norm_two",
    )(t_rank, x, keep, came, far, gain)


def middle_back_kernel(*refs):
    terms, tails, refs = refs[:6], refs[6:9], refs[9:]
    (mix_ref, router_ref, middle_ref, cot_ref, gain_ref,
     dmid_ref, db_ref, dlog_ref, gain2_ref, dl_ref) = refs
    step = pl.program_id(0)
    rb, width = middle_ref.shape
    experts, quarter = mix_ref.shape

    @pl.when(step == 0)
    def _():
        tail = sum(t[...].astype(f32) for t in tails)
        extra = tail.shape[0] // 2
        tail = tail[:extra] + tail[extra:]
        d_mix = jnp.concatenate(
            [tail[:, j * quarter:(j + 1) * quarter] for j in range(-(-experts // extra))], axis=0
        )[:experts]
        mix = mix_ref[...]
        d_logits = mix * (d_mix - jnp.sum(mix * d_mix, axis=0, keepdims=True))
        d_logits = jnp.transpose(d_logits).astype(bf16)
        dlog_ref[...] = d_logits
        dl_ref[...] = d_logits
        gain2_ref[...] = jnp.zeros_like(gain2_ref)

    first = [t[...].astype(f32) for t in terms[:3]]
    second = [t[...].astype(f32) for t in terms[3:]]
    routed = jnp.where(step < pl.num_programs(0) // 2, sum(first), sum(second))
    d_logits = dl_ref[pl.ds(pl.multiple_of(step * rb, rb), rb), :]
    d_normed = routed + mm(d_logits, router_ref[...])
    middle = middle_ref[...]
    inv = lax.rsqrt(jnp.mean(middle * middle, axis=-1, keepdims=True) + EPS)
    gain2_ref[...] += jnp.sum(d_normed * middle * inv, axis=0, keepdims=True)
    scaled = d_normed * gain_ref[...].astype(f32)
    d_middle = (
        cot_ref[...].astype(f32)
        + inv * scaled
        - middle * (inv * inv * inv * jnp.mean(scaled * middle, axis=-1, keepdims=True))
    )
    dmid_ref[...] = d_middle
    db_ref[...] = d_middle.astype(bf16)


def middle_back_call(terms, mix_t, router_t, middle, cotangent, gain):
    quarter, width = middle.shape
    experts = mix_t.shape[0]
    half = quarter // 2
    tail = terms[0][1].shape[0] - half
    rb = half // 4
    row = pl.BlockSpec((rb, width), lambda s: (s, 0))
    low = pl.BlockSpec((rb, width), lambda s: (jnp.minimum(s, 3), 0))
    high = pl.BlockSpec((rb, width), lambda s: (jnp.maximum(s - 4, 0), 0))
    end = pl.BlockSpec((tail, width), lambda s: (half // tail, 0))
    whole = lambda shape: pl.BlockSpec(shape, lambda s: (0,) * len(shape))
    firsts, seconds = [t[0] for t in terms], [t[1] for t in terms]
    return pl.pallas_call(
        middle_back_kernel,
        grid=(8,),
        in_specs=[low] * 3 + [high] * 3 + [end] * 3
        + [whole((experts, quarter)), whole((experts, width)), row, row, whole((1, width))],
        out_specs=[row, row, whole((quarter, experts)), whole((1, width))],
        out_shape=[
            jax.ShapeDtypeStruct((quarter, width), f32),
            jax.ShapeDtypeStruct((quarter, width), bf16),
            jax.ShapeDtypeStruct((quarter, experts), bf16),
            jax.ShapeDtypeStruct((1, width), f32),
        ],
        scratch_shapes=[pltpu.VMEM((quarter, experts), bf16)],
        compiler_params=params(16),
        cost_estimate=takes(7),
        name="middle_back",
    )(*firsts, *seconds, *seconds, mix_t, router_t, middle, cotangent, gain)


def in_first_half():
    return pl.program_id(0) < pl.num_programs(0) // 2


def two_sums_kernel(first, wait_ref, a_ref, b_ref, p0_ref, p1_ref, m0_ref, m1_ref, pa_ref, mb_ref):
    plus = jnp.where(in_first_half(), p0_ref[...], p1_ref[...]).astype(f32)
    minus = jnp.where(in_first_half(), m0_ref[...], m1_ref[...]).astype(f32)
    a, b = a_ref[...].astype(f32), b_ref[...].astype(f32)
    if first:
        a, b = jnp.where(in_first_half(), a, 0.0), jnp.where(in_first_half(), 0.0, b)
    pa_ref[...] = (a + plus).astype(bf16)
    mb_ref[...] = (b + minus).astype(bf16)


def half_specs(rb, width):
    return (
        pl.BlockSpec((rb, width), lambda s, *_: (s, 0)),
        pl.BlockSpec((rb, width), lambda s, *_: (jnp.minimum(s, 3), 0)),
        pl.BlockSpec((rb, width), lambda s, *_: (jnp.maximum(s - 4, 0), 0)),
    )


def two_sums_call(wait, a, b, plus, minus, first):
    rows, width = 2 * plus[0].shape[0], plus[0].shape[1]
    row, low, high = half_specs(rows // 8, width)
    return pl.pallas_call(
        functools.partial(two_sums_kernel, first),
        grid_spec=pltpu.PrefetchScalarGridSpec(
            num_scalar_prefetch=1,
            grid=(8,),
            in_specs=[low if first else row, high if first else row, low, high, low, high],
            out_specs=[row, row],
        ),
        out_shape=[jax.ShapeDtypeStruct((rows, width), bf16)] * 2,
        compiler_params=params(10),
        cost_estimate=takes(4),
        name="two_sums",
    )(wait.astype(i32)[None], a, b, *plus, *minus)


def layer_out_kernel(middle_ref, first_ref, second_ref, a_ref, b_ref, out_ref):
    own = jnp.where(in_first_half(), first_ref[...], second_ref[...]).astype(f32)
    out_ref[...] = (
        middle_ref[...] + own + a_ref[...].astype(f32) + b_ref[...].astype(f32)
    ).astype(bf16)


def layer_out_call(middle, own, a, b):
    quarter, width = middle.shape
    row, low, high = half_specs(quarter // 8, width)
    return pl.pallas_call(
        layer_out_kernel,
        grid=(8,),
        in_specs=[row, low, high, row, row],
        out_specs=row,
        out_shape=jax.ShapeDtypeStruct((quarter, width), bf16),
        compiler_params=params(10),
        cost_estimate=takes(4),
        name="layer_out",
    )(middle, *own, a, b)


def input_back_kernel(at_ref, keep_ref, came_ref, far_ref, dmid_ref, x_ref, gain_ref, out_ref):
    d_normed = keep_ref[...].astype(f32) + came_ref[...].astype(f32) + far_ref[...].astype(f32)
    x = x_ref[...].astype(f32)
    inv = lax.rsqrt(jnp.mean(x * x, axis=-1, keepdims=True) + EPS)
    scaled = d_normed * gain_ref[...].astype(f32)
    out_ref[...] = (
        dmid_ref[...]
        + inv * scaled
        - x * (inv * inv * inv * jnp.mean(scaled * x, axis=-1, keepdims=True))
    )


def input_back_call(t_rank, keep, came, far, d_middle, x, gain):
    quarter, width = d_middle.shape
    rb = quarter // 8
    row = pl.BlockSpec((rb, width), lambda s, t: (s, 0))
    behind = pl.BlockSpec((rb, width), lambda s, t: (8 + s, 0))
    return pl.pallas_call(
        input_back_kernel,
        grid_spec=pltpu.PrefetchScalarGridSpec(
            num_scalar_prefetch=1,
            grid=(8,),
            in_specs=[
                behind, behind, row, row,
                pl.BlockSpec((rb, width), lambda s, t: (8 * t[0] + s, 0)),
                pl.BlockSpec((1, width), lambda s, t: (0, 0)),
            ],
            out_specs=row,
        ),
        out_shape=jax.ShapeDtypeStruct((quarter, width), f32),
        compiler_params=params(10),
        cost_estimate=takes(6),
        name="input_back",
    )(t_rank, keep, came, far, d_middle, x, gain)


def ring_of(n):
    return list(range(0, n, 2)) + list(range(n - 1, 0, -2))


def index_at(place, n):
    return jnp.where(place < n // 2, 2 * place, 2 * n - 1 - 2 * place)


def ring_moves(n):
    ring = ring_of(n)
    ahead = [(ring[p], ring[(p + 1) % n]) for p in range(n)]
    return ahead, [(b, a) for a, b in ahead]


def add_low(a, b, wait=0.0):
    return (a.astype(f32) + jnp.asarray(b).astype(f32) + wait).astype(bf16)


class RingSum:

    def __init__(self, own, parts, n):
        self.own, self.parts, self.half = own, parts, n // 2
        self.ways = ring_moves(n)
        self.long, self.short = [None, None], [None, None]
        self.rounds = 0

    def term(self, distance, way, half):
        if distance == self.half:
            return self.parts[-1][0][half]
        return self.parts[distance - 1][1 - way][half]

    def round(self, wait=0.0):
        r = self.rounds
        self.rounds += 1
        sums = []
        for held, hop, distance, turn in (
            (self.short, r, self.half - 1 - r, 1),
            (self.long, r - 1, self.half + 1 - r, 0),
        ):
            if hop < 0 or distance < 1:
                continue
            for way in range(2):
                t = self.term(distance, way, (way + turn) % 2)
                if hop > 0:
                    t = add_low(held[way], t, wait)
                    sums.append(t)
                held[way] = lax.ppermute(t, "dp", self.ways[way])
        return sums

    def terms(self):
        a, b = self.long, self.short
        return [tuple(self.own), (a[0], b[0]), (b[1], a[1])]


CORE = [(0, 1), (1, 0), (2, 3), (3, 2)]
CHIP = [(0, 2), (2, 0), (1, 3), (3, 1)]


def to_core(a):
    return lax.ppermute(a, "tensor", CORE)


def to_chip(a):
    return lax.ppermute(a, "tensor", CHIP)


def zero_of(a):
    while a.ndim > 2:
        a = a[0]
    return jnp.minimum(jnp.abs(a[0, 0].astype(f32)), 0.0)


def mark(a):
    while a.ndim > 2:
        a = a[0]
    return zero_of(a)


def after(first, then):
    return lax.optimization_barrier((then, first))[0]


def per_device(layer_input, segments, routes, norm1_gain, w_query, w_key, w_value, w_output,
               norm2_gain, router, w_gate, w_up, w_down, cotangent, n_dp):
    tokens_dev, width = layer_input.shape
    quarter, top_count = routes.shape
    experts = router.shape[1]
    local = w_gate.shape[0]
    cap = quarter * top_count * 5 // (4 * experts)
    hidden = w_gate.shape[2]
    t_rank = lax.axis_index("tensor")
    d_rank = lax.axis_index("dp")
    place = jnp.where(d_rank % 2 == 0, d_rank // 2, n_dp - 1 - d_rank // 2)
    ringed = n_dp in (4, 6, 8)
    cos, sin = rope_tables()

    hot_t = jnp.any(
        routes.T[:, None, :] == jnp.arange(experts, dtype=i32)[None, :, None], axis=0
    )
    before = (jnp.arange(quarter)[:, None] < jnp.arange(quarter)[None, :]).astype(bf16)
    rank_t = jnp.dot(hot_t.astype(bf16), before, preferred_element_type=f32)
    rank_t = jnp.where(hot_t, rank_t, -1.0).astype(bf16)
    per_row = width // quarter
    extra = 16 * -(-experts // (16 * per_row))
    rank_rows = jnp.concatenate(
        [rank_t, jnp.full((extra * per_row - experts, quarter), -1.0, bf16)], axis=0
    ).reshape(per_row, extra, quarter)
    rank_rows = jnp.concatenate([rank_rows[j] for j in range(per_row)], axis=1)
    payload = jnp.concatenate([cotangent, rank_rows], axis=0)
    router_t = router.T
    ahead, behind = ring_moves(n_dp)
    zero = jnp.zeros((), i32)
    own_at = t_rank.astype(i32)[None]
    mate, other, cross = t_rank ^ 1, t_rank ^ 2, t_rank ^ 3
    quarters = jnp.stack([cross, mate, other, t_rank]).astype(i32)
    pairs_of = lambda *ts: jnp.stack([2 * t + j for t in ts for j in range(2)]).astype(i32)

    if ringed:
        a = b = payload
        grads_from = []
        for _ in range(n_dp // 2 - 1):
            a, b = lax.ppermute(a, "dp", ahead), lax.ppermute(b, "dp", behind)
            grads_from.append((a, b))
        stage = [after(g, zero) for g in grads_from]
    else:
        stage = [zero] * 3
    normed1, q, k, v, kt = qkv_call(
        layer_input, after(payload, norm1_gain[None, :]), w_query, w_key, w_value, cos, sin
    )
    seg_col, seg_row = segments[:, None], segments[None, :]
    heads, lse, send_a, keep_a = attend_call(
        pairs_of(cross, other), q, k, v, seg_col, seg_row, w_output
    )
    if ringed:
        send_a, grads_from[0] = lax.optimization_barrier((send_a, grads_from[0]))
    sum_a = add_low(keep_a, to_core(send_a))
    far = to_chip(sum_a)
    heads, lse, send_b, keep_b = attend_call(
        after(sum_a, pairs_of(mate, t_rank)),
        q, k, v, seg_col, seg_row, w_output, held=(heads, lse),
    )
    came_b = jnp.concatenate([to_core(send_b[:QB]), to_core(send_b[QB:])], axis=0)
    middle, *normed2 = norm_two_call(
        own_at + stage[1], layer_input, keep_b, came_b, far, norm2_gain[None, :]
    )

    base = (d_rank * local).astype(i32)[None]
    run = lambda base, xs, cs, at, of, held: expert_call(
        base, xs, cs, router_t, w_gate, w_up, w_down, cap, at, of, held
    )

    def own_mixing(rows):
        logits = jnp.concatenate([mm(router_t, r, NT) for r in rows], axis=1)
        return jax.nn.softmax(jnp.where(hot_t, logits, -jnp.inf), axis=0)

    def core_sum(parts, wait):
        send, keep = parts
        came = to_core(send)
        away = add_low(keep[0], came[0], wait)
        return keep[1], came[1], away

    def chip_sum(sums, wait):
        keep, came, away = sums
        return keep.astype(f32) + came.astype(f32) + to_chip(away).astype(f32) + wait

    if ringed:
        own = tuple(normed2)
        step = lambda rows, way: tuple(lax.ppermute(r, "dp", way) for r in rows)
        xs = [step(own, ahead), step(own, behind)]
        (out_own,), (back_own,), held = run(base, [own], [payload], n_dp - 1, n_dp, None)
        outs, backs, last = [], [], out_own
        cut = payload.shape[0] // 32 * 16
        for j in range(n_dp // 2):
            cs = grads_from[j]
            if j < n_dp // 2 - 1:
                at = j
                a, b = after(last, xs)
                if j < n_dp // 2 - 2:
                    later = [step(a, ahead), step(b, behind)]
                else:
                    later = [step(a[:1], ahead) + step(b[1:], behind)]
            else:
                at = n_dp - 2
            wait = after(grads_from[-1], zero) if j == n_dp // 2 - 2 else zero
            if j == max(n_dp // 2 - 3, 0):
                a, b = after(last, grads_from[-1])
                a, b = lax.ppermute(a[:cut], "dp", ahead), lax.ppermute(b[cut:], "dp", behind)
                grads_from.append((jnp.concatenate([a, b], axis=0),))
            o, b, held = run(base + wait, xs, cs, at, n_dp, held)
            outs.append(o)
            backs.append(b)
            last, xs = o, later
        back = RingSum(back_own, backs, n_dp)
        back.round()
        sums = back.round(mark(backs[-1][0][0]))
        mix_t = own_mixing(after(sums, own))
        grad_of = lambda i, j: weight_grad_call(
            quarters + after(sums, zero), held[i], held[j]
        )
        gate_parts = grad_of(0, 3)
        sums = back.round(mark(gate_parts[1]))
        up_parts = grad_of(0, 4)
        end = mark(up_parts[1])
        sums = back.round(end)
        gate_sum = core_sum(gate_parts, end)
        down_parts = weight_grad_call(
            quarters + after(sums, zero) + zero_of(gate_sum[2]).astype(i32), held[2], held[1], True
        )
        end = mark(down_parts[1])
        sums = back.round(end)
        gate_grad = chip_sum(gate_sum, end)
        gate_done = zero_of(gate_grad)
        routed = back.terms()
    else:
        grads_all = lax.all_gather(payload, "dp", axis=0)
        rows_all = lax.all_gather(jnp.concatenate(normed2, axis=0), "dp", axis=0)
        halves = lambda a: (a[:quarter // 2], a[quarter // 2:])

        def two(sums, pair_rows):
            x, c = pair_rows
            o, b, held = run(base, [halves(x[0]), halves(x[1])], [c[0], c[1]], 0, 2, None)
            grads = [
                list(weight_grad_call(quarters, held[i], held[j], i == 2))
                for i, j in ((0, 3), (0, 4), (2, 1))
            ]
            sums = jax.tree.map(lambda t, g: t + g.astype(f32), sums, grads)
            join = lambda a: jnp.stack([jnp.concatenate(h, axis=0) for h in a])
            return sums, (join(o), join(b))

        pairs = lambda a: a.reshape((n_dp // 2, 2) + a.shape[1:])
        none = jnp.zeros((2, local, width // 4, hidden), f32)
        none = [[none] * 2, [none] * 2, [none.transpose(0, 1, 3, 2)] * 2]
        grads, (outs, backs) = lax.scan(
            two, none, (pairs(rows_all), pairs(grads_all))
        )
        gate_parts, up_parts, down_parts = jax.tree.map(lambda a: a.astype(bf16), grads)
        gate_grad = chip_sum(core_sum(gate_parts, 0.0), 0.0)
        gate_done = 0.0
        scatter = lambda a: lax.psum_scatter(
            a.reshape(-1, width), "dp", scatter_dimension=0, tiled=True
        )
        mix_t = own_mixing(normed2)
        empty = jax.tree.map(jnp.zeros_like, halves(scatter(backs)))
        routed = [halves(scatter(backs)), empty, empty]

    d_middle, db_own, d_logits, second_gain_part = middle_back_call(
        routed, mix_t, router_t, middle, cotangent,
        (norm2_gain.astype(f32) + gate_done).astype(bf16)[None, :],
    )

    db_mate = to_core(db_own)
    other_first, other_second = to_chip(db_own[:QB]), to_chip(db_own[QB:])
    common = (q, k, v, kt, seg_row, seg_col, heads, lse)
    if ringed:
        out_a, out_b = after(sums, outs[-1][0])
        out_a, out_b = lax.ppermute(out_a, "dp", ahead), lax.ppermute(out_b, "dp", behind)

        def out_step(a, b, j, wait):
            minus, plus = outs[j - 1]
            a, b = two_sums_call(wait, a, b, plus, minus, j == n_dp // 2 - 1)
            return lax.ppermute(a, "dp", ahead), lax.ppermute(b, "dp", behind), (a, b)

        steps = list(range(n_dp // 2 - 1, 0, -1))
    else:
        out_own = halves(scatter(outs))
        out_a = out_b = jnp.zeros((quarter, width), bf16)
        out_step = lambda a, b, j, wait: (a, b, zero)
        steps = [0, 0, 0]
    out_a, out_b, sums = out_step(out_a, out_b, steps[0], zero_of(db_own))
    dq, dk, dv = attend_back_call(
        pairs_of(t_rank, mate) + after(sums, zero) + zero_of(other_first).astype(i32), *common, db_own, db_mate, w_output, cos, sin
    )
    end = mark(dq)
    db_other = add_low(jnp.concatenate([other_first, other_second], axis=0), end)
    up_sum = core_sum(up_parts, end)
    out_a, out_b, sums = out_step(out_a, out_b, steps[1], end)
    db_cross = to_core(db_other)
    dq, dkv = attend_back_call(
        pairs_of(other, cross) + after(sums, zero)
        + zero_of(up_sum[2]).astype(i32),
        *common, db_other, db_cross, w_output,
        cos, sin, held=(dq, dk, dv),
    )
    sums = zero
    for j in steps[2:]:
        out_a, out_b, sums = out_step(out_a, out_b, j, zero_of(dkv))
    up_grad = chip_sum(up_sum, zero_of(dkv))
    packed_dense = dense_grad_call(
        jnp.stack([t_rank, mate, other, cross]).astype(i32) + after(sums, zero)
        + zero_of(up_grad).astype(i32),
        normed1, dq, dkv, (db_own, db_mate, db_other, db_cross), heads, normed2, d_logits,
        second_gain_part, norm1_gain[None, :], (w_query, w_key, w_value),
    )
    down_sum = core_sum(down_parts, zero_of(packed_dense))
    send, keep = qkv_back_call(
        pairs_of(cross, mate, other, t_rank) + after(packed_dense, zero),
        dq, dkv, w_query, w_key, w_value,
    )
    came = to_core(send)
    sum_in = add_low(keep[:quarter], came[:quarter])
    far = to_chip(sum_in)
    down_grad = chip_sum(down_sum, zero_of(sum_in))

    input_grad = input_back_call(
        own_at, keep, came, far, d_middle, layer_input, norm1_gain[None, :]
    )

    dense_sum = lax.psum_scatter(
        packed_dense, "dp", scatter_dimension=0, tiled=True
    ).astype(f32)
    q_cols, kv_cols = w_query.shape[1], w_key.shape[1]
    query_grad = dense_sum[:, :q_cols]
    key_grad = dense_sum[:, q_cols:q_cols + kv_cols]
    value_grad = dense_sum[:, q_cols + kv_cols:q_cols + 2 * kv_cols]
    cols = 2 * (q_cols + kv_cols)
    output_grad = jnp.transpose(dense_sum[:, q_cols + 2 * kv_cols:cols])
    rows = width // n_dp
    small = dense_sum[:, cols:cols + experts + 2] + zero_of(input_grad)
    small = small + to_core(small)
    small = small + to_chip(small)
    small = lax.dynamic_slice_in_dim(small, t_rank * (rows // 4), rows // 4)

    layer_out = layer_out_call(middle, out_own, out_a, out_b)
    return (
        layer_out,
        input_grad,
        small[:, experts + 1],
        query_grad,
        key_grad,
        value_grad,
        output_grad,
        small[:, experts],
        small[:, :experts],
        gate_grad,
        up_grad,
        down_grad,
    )


def solution(mesh):
    both = ("dp", "tensor")
    return jax.shard_map(
        functools.partial(per_device, n_dp=mesh.shape["dp"]),
        mesh=mesh,
        in_specs=(
            P("dp", None), P("dp"), P(both, None), P(),
            P(None, "tensor"), P(None, "tensor"), P(None, "tensor"), P("tensor", None),
            P(), P(), P("dp", None, None), P("dp", None, None), P("dp", None, None),
            P(both, None),
        ),
        out_specs=(
            P(both, None), P(both, None), P(both), P("dp", "tensor"), P("dp", "tensor"),
            P("dp", "tensor"), P("tensor", "dp"), P(both), P(both, None),
            P("dp", "tensor", None), P("dp", "tensor", None), P("dp", None, "tensor"),
        ),
        check_vma=False,
    )
```

```python
import functools

import jax
import jax.numpy as jnp
import numpy as np
from jax import lax
from jax.experimental import pallas as pl
from jax.experimental.pallas import tpu as pltpu
from jax.sharding import PartitionSpec as P

HD = 64
WINDOW = 1024
SEQ = 2048
QB = 256
EPS = 1e-05
NEG = -1e30
MIB = 1 << 20
f32 = jnp.float32
bf16 = jnp.bfloat16
i32 = jnp.int32

NT = (((1,), (1,)), ((), ()))
TN = (((0,), (0,)), ((), ()))
NN = (((1,), (0,)), ((), ()))


def mm(a, b, dims=NN):
    return lax.dot_general(a, b, dims, preferred_element_type=f32)


def params(mib, n=1):
    return pltpu.CompilerParams(
        vmem_limit_bytes=mib * MIB, dimension_semantics=("arbitrary",) * n
    )


WEIGHT = 1.0


def takes(us):
    return pl.CostEstimate(
        flops=int(us * WEIGHT * 1.153e9), bytes_accessed=1_000_000, transcendentals=0
    )


def rope_tables():
    half = HD // 2
    freq = (10000.0 ** (-np.arange(half, dtype=np.float32) / half)).astype(np.float32)
    angles = (np.arange(SEQ, dtype=np.float32)[:, None] * freq[None, :]).astype(np.float32)
    cos, sin = np.cos(angles), np.sin(angles)
    return (
        np.concatenate([cos] * 4, axis=1).astype(np.float32),
        np.concatenate([-sin, sin] * 2, axis=1).astype(np.float32),
    )


def swap_halves(u):
    lane = lax.broadcasted_iota(i32, u.shape, 1) % HD
    return jnp.where(lane < HD // 2, pltpu.roll(u, 2 * HD - HD // 2, 1), pltpu.roll(u, HD // 2, 1))


def qkv_kernel(x_ref, gain_ref, wq_ref, wk_ref, wv_ref, cos_ref, sin_ref,
               n_ref, q_ref, k_ref, v_ref, kt_ref):
    x = x_ref[...].astype(f32)
    inv = lax.rsqrt(jnp.mean(x * x, axis=-1, keepdims=True) + EPS)
    normed = (x * inv * gain_ref[...].astype(f32)).astype(bf16)
    n_ref[...] = normed
    cos, sin = cos_ref[...], sin_ref[...]
    q = mm(normed, wq_ref[...])
    for c in range(q.shape[1] // 128):
        u = q[:, 128 * c:128 * (c + 1)]
        r = ((u * cos + swap_halves(u) * sin) * HD ** (-0.5)).astype(bf16)
        q_ref[2 * c] = r[:, :HD]
        q_ref[2 * c + 1] = r[:, HD:]
    k = mm(normed, wk_ref[...])
    v = mm(normed, wv_ref[...])
    for c in range(k.shape[1] // 128):
        u = k[:, 128 * c:128 * (c + 1)]
        r = u * cos + swap_halves(u) * sin
        rb = r.astype(bf16)
        k_ref[2 * c] = rb[:, :HD]
        k_ref[2 * c + 1] = rb[:, HD:]
        rt = jnp.transpose(r).astype(bf16)
        kt_ref[2 * c] = rt[:HD]
        kt_ref[2 * c + 1] = rt[HD:]
        vb = v[:, 128 * c:128 * (c + 1)].astype(bf16)
        v_ref[2 * c] = vb[:, :HD]
        v_ref[2 * c + 1] = vb[:, HD:]


def qkv_call(x, gain, wq, wk, wv, cos, sin):
    rows, width = x.shape
    rb = 512
    qc, kc = wq.shape[1], wk.shape[1]
    qh, kh = qc // HD, kc // HD
    per_seq = SEQ // rb
    whole = lambda shape: pl.BlockSpec(shape, lambda i: (0,) * len(shape))
    return pl.pallas_call(
        qkv_kernel,
        grid=(rows // rb,),
        in_specs=[
            pl.BlockSpec((rb, width), lambda i: (i, 0)),
            whole((1, width)), whole((width, qc)), whole((width, kc)), whole((width, kc)),
            pl.BlockSpec((rb, 128), lambda i: (i % per_seq, 0)),
            pl.BlockSpec((rb, 128), lambda i: (i % per_seq, 0)),
        ],
        out_specs=[
            pl.BlockSpec((rb, width), lambda i: (i, 0)),
            pl.BlockSpec((qh, rb, HD), lambda i: (0, i, 0)),
            pl.BlockSpec((kh, rb, HD), lambda i: (0, i, 0)),
            pl.BlockSpec((kh, rb, HD), lambda i: (0, i, 0)),
            pl.BlockSpec((kh, HD, rb), lambda i: (0, 0, i)),
        ],
        out_shape=[
            jax.ShapeDtypeStruct((rows, width), bf16),
            jax.ShapeDtypeStruct((qh, rows, HD), bf16),
            jax.ShapeDtypeStruct((kh, rows, HD), bf16),
            jax.ShapeDtypeStruct((kh, rows, HD), bf16),
            jax.ShapeDtypeStruct((kh, HD, rows), bf16),
        ],
        compiler_params=params(48),
        cost_estimate=takes(99),
        name="norm_qkv",
    )(x, gain, wq, wk, wv, cos, sin)


def window_blocks():
    return WINDOW // QB + 1


def on_block(i, body):
    most = window_blocks()
    for j in range(most - 1):
        pl.when(i == j)(functools.partial(body, j + 1, 0))
    pl.when(i >= most - 1)(
        lambda: body(most, pl.multiple_of((i - (most - 1)) * QB, QB))
    )


def attend_kernel(order_ref, q_ref, k_ref, v_ref, segq_ref, segk_ref, wo_ref, *rest):
    heads_ref, lse_ref, send_ref, keep_ref, bias_ref = rest[-5:]
    step = pl.program_id(0)
    i = order_ref[step]
    qh, kh = q_ref.shape[0], k_ref.shape[0]
    group = qh // kh

    def body(blocks, start):
        span = blocks * QB
        segq = segq_ref[...]
        segq = jnp.where(segq == 0, -1, segq)
        row = lax.broadcasted_iota(i32, (QB, QB), 0)
        col = lax.broadcasted_iota(i32, (QB, QB), 1)
        for j in range(blocks):
            same = segk_ref[:, pl.ds(start + j * QB, QB)] == segq
            if j == blocks - 1:
                same = (same & (col <= row)) | (col == row)
            elif blocks == window_blocks() and j == 0:
                same = same & (row < col)
            bias_ref[:, j * QB:(j + 1) * QB] = jnp.where(same, 0.0, NEG)
        lane = lax.broadcasted_iota(i32, (QB, 128), 1)
        logs = jnp.zeros((QB, 128), f32)
        outs = []
        for g in range(kh):
            q = q_ref[g * group:(g + 1) * group].reshape(group * QB, HD)
            k = k_ref[g, pl.ds(start, span), :]
            v = v_ref[g, pl.ds(start, span), :]
            s = mm(q, k, NT).reshape(group, QB, span) + bias_ref[:, :span][None]
            top = jnp.max(s, axis=-1, keepdims=True)
            p = jnp.exp(s - top)
            total = jnp.sum(p, axis=-1, keepdims=True)
            o = mm(p.astype(bf16).reshape(group * QB, span), v).reshape(group, QB, HD)
            o = (o * (1.0 / total)).astype(bf16)
            log = top + jnp.log(total)
            for h in range(group):
                outs.append(o[h])
                logs = jnp.where(lane == g * group + h, log[h], logs)
        heads = jnp.concatenate(outs, axis=1)
        heads_ref[...] = heads
        lse_ref[...] = jnp.transpose(logs)[:lse_ref.shape[0]]
        part = mm(heads, wo_ref[...]).astype(bf16)

        @pl.when(step < 2)
        def _():
            send_ref[...] = part

        @pl.when(step >= 2)
        def _():
            keep_ref[...] = part

    on_block(i, body)


def attend_call(order, q, k, v, seg_col, seg_row, wo, held=None):
    qh, rows, _ = q.shape
    kh = k.shape[0]
    width = wo.shape[1]
    lse_rows = -(-qh // 8) * 8
    in_specs = [
        pl.BlockSpec((qh, QB, HD), lambda s, o: (0, o[s], 0)),
        pl.BlockSpec((kh, rows, HD), lambda s, o: (0, 0, 0)),
        pl.BlockSpec((kh, rows, HD), lambda s, o: (0, 0, 0)),
        pl.BlockSpec((QB, 1), lambda s, o: (o[s], 0)),
        pl.BlockSpec((1, rows), lambda s, o: (0, 0)),
        pl.BlockSpec((qh * HD, width), lambda s, o: (0, 0)),
    ]
    args = [q, k, v, seg_col, seg_row, wo]
    aliases = {}
    if held is not None:
        aliases = {1 + len(args): 0, 2 + len(args): 1}
        args += list(held)
        in_specs += [pl.BlockSpec(memory_space=pl.ANY)] * 2
    return pl.pallas_call(
        attend_kernel,
        grid_spec=pltpu.PrefetchScalarGridSpec(
            num_scalar_prefetch=1,
            grid=(4,),
            in_specs=in_specs,
            out_specs=[
                pl.BlockSpec((QB, qh * HD), lambda s, o: (o[s], 0)),
                pl.BlockSpec((lse_rows, QB), lambda s, o: (0, o[s])),
                pl.BlockSpec((QB, width), lambda s, o: (jnp.minimum(s, 1), 0)),
                pl.BlockSpec((QB, width), lambda s, o: (jnp.maximum(s - 2, 0), 0)),
            ],
            scratch_shapes=[pltpu.VMEM((QB, window_blocks() * QB), f32)],
        ),
        out_shape=[
            jax.ShapeDtypeStruct((rows, qh * HD), bf16),
            jax.ShapeDtypeStruct((lse_rows, rows), f32),
            jax.ShapeDtypeStruct((2 * QB, width), bf16),
            jax.ShapeDtypeStruct((2 * QB, width), bf16),
        ],
        input_output_aliases=aliases,
        compiler_params=params(56),
        cost_estimate=takes(1),
        name="attend",
    )(order, *args)


def attend_back_kernel(last, order_ref, q_ref, k_ref, v_ref, kt_ref, segq_ref, segk_ref,
                       heads_ref, lse_ref, dba_ref, dbb_ref, wo_ref, cos_ref, sin_ref, *rest):
    if last:
        (cosk_ref, sink_ref, dk_in, dv_in, _, dq_ref, dkv_ref,
         bias_ref, dk_ref, dv_ref, p_ref, ds_ref) = rest
    else:
        dq_ref, dk_ref, dv_ref, bias_ref, p_ref, ds_ref = rest
    step = pl.program_id(0)
    i = order_ref[step]
    qh, kh = q_ref.shape[0], k_ref.shape[0]
    group = qh // kh

    @pl.when(step == 0)
    def _():
        dk_ref[...] = dk_in[...] if last else jnp.zeros_like(dk_ref)
        dv_ref[...] = dv_in[...] if last else jnp.zeros_like(dv_ref)

    def body(blocks, start):
        span = blocks * QB
        segq = segq_ref[...]
        segq = jnp.where(segq == 0, -1, segq)
        row = lax.broadcasted_iota(i32, (QB, QB), 1)
        col = lax.broadcasted_iota(i32, (QB, QB), 0)
        for j in range(blocks):
            same = segk_ref[pl.ds(start + j * QB, QB), :] == segq
            if j == blocks - 1:
                same = (same & (col <= row)) | (col == row)
            elif blocks == window_blocks() and j == 0:
                same = same & (row < col)
            bias_ref[j * QB:(j + 1) * QB, :] = jnp.where(same, 0.0, NEG)
        db = jnp.where(step < 2, dba_ref[...], dbb_ref[...])
        heads = heads_ref[...]
        dh = mm(db, wo_ref[...], NT).astype(bf16)
        prod = jnp.transpose(dh.astype(f32) * heads.astype(f32))
        dqs = []
        for g in range(kh):
            k = k_ref[g, pl.ds(start, span), :]
            v = v_ref[g, pl.ds(start, span), :]
            dos = []
            for h in range(group):
                at = g * group + h
                do = dh[:, at * HD:(at + 1) * HD]
                dos.append(do)
                delta = jnp.sum(prod[at * HD:(at + 1) * HD], axis=0, keepdims=True)
                s = mm(k, q_ref[at], NT) + bias_ref[:span]
                p = jnp.exp(s - lse_ref[at:at + 1, :])
                dp = mm(v, do, NT)
                p_ref[:span, h * QB:(h + 1) * QB] = p.astype(bf16)
                ds_ref[:span, h * QB:(h + 1) * QB] = (p * (dp - delta)).astype(bf16)
            q = q_ref[g * group:(g + 1) * group].reshape(group * QB, HD)
            dk_ref[g, pl.ds(start, span), :] += mm(ds_ref[:span], q)
            dv_ref[g, pl.ds(start, span), :] += mm(p_ref[:span], jnp.concatenate(dos, axis=0))
            dq = mm(kt_ref[g, :, pl.ds(start, span)], ds_ref[:span]) * HD ** (-0.5)
            for h in range(group):
                dqs.append(dq[:, h * QB:(h + 1) * QB])
        dq = jnp.transpose(jnp.concatenate(dqs, axis=0))
        cos, sin = cos_ref[...], sin_ref[...]
        for c in range(dq.shape[1] // 128):
            u = dq[:, 128 * c:128 * (c + 1)]
            dq_ref[:, 128 * c:128 * (c + 1)] = (u * cos - swap_halves(u) * sin).astype(bf16)

    on_block(i, body)

    if last:
        @pl.when(step == pl.num_programs(0) - 1)
        def _():
            for c in range(kh // 2):
                u = jnp.concatenate([dk_ref[2 * c], dk_ref[2 * c + 1]], axis=1)
                u = u * cosk_ref[...] - swap_halves(u) * sink_ref[...]
                dkv_ref[:, 128 * c:128 * (c + 1)] = u.astype(bf16)
                w = jnp.concatenate([dv_ref[2 * c], dv_ref[2 * c + 1]], axis=1)
                dkv_ref[:, (kh // 2 + c) * 128:(kh // 2 + c + 1) * 128] = w.astype(bf16)


def attend_back_call(order, q, k, v, kt, seg_row, seg_col, heads, lse, db_a, db_b, wo, cos, sin,
                     held=None):
    qh, rows, _ = q.shape
    kh = k.shape[0]
    width = wo.shape[1]
    span = window_blocks() * QB
    group = qh // kh
    last = held is not None
    whole = lambda shape: pl.BlockSpec(shape, lambda s, o: (0,) * len(shape))
    in_specs = [
        pl.BlockSpec((qh, QB, HD), lambda s, o: (0, o[s], 0)),
        whole((kh, rows, HD)), whole((kh, rows, HD)), whole((kh, HD, rows)),
        pl.BlockSpec((1, QB), lambda s, o: (0, o[s])),
        whole((rows, 1)),
        pl.BlockSpec((QB, qh * HD), lambda s, o: (o[s], 0)),
        pl.BlockSpec((lse.shape[0], QB), lambda s, o: (0, o[s])),
        pl.BlockSpec((QB, width), lambda s, o: (jnp.minimum(s, 1), 0)),
        pl.BlockSpec((QB, width), lambda s, o: (jnp.maximum(s - 2, 0), 0)),
        whole((qh * HD, width)),
        pl.BlockSpec((QB, 128), lambda s, o: (o[s], 0)),
        pl.BlockSpec((QB, 128), lambda s, o: (o[s], 0)),
    ]
    args = [q, k, v, kt, seg_row, seg_col, heads, lse, db_a, db_b, wo, cos, sin]
    out_specs = [pl.BlockSpec((QB, qh * HD), lambda s, o: (o[s], 0))]
    out_shape = [jax.ShapeDtypeStruct((rows, qh * HD), bf16)]
    scratch = [pltpu.VMEM((span, QB), f32)]
    aliases = {}
    if last:
        dq, dk, dv = held
        aliases = {1 + len(args) + 4: 0}
        args += [cos, sin, dk, dv, dq]
        in_specs += [whole((rows, 128)), whole((rows, 128)), whole((kh, rows, HD)),
                     whole((kh, rows, HD)), pl.BlockSpec(memory_space=pl.ANY)]
        out_specs += [whole((rows, 2 * kh * HD))]
        out_shape += [jax.ShapeDtypeStruct((rows, 2 * kh * HD), bf16)]
        scratch += [pltpu.VMEM((kh, rows, HD), f32)] * 2
    else:
        out_specs += [whole((kh, rows, HD))] * 2
        out_shape += [jax.ShapeDtypeStruct((kh, rows, HD), f32)] * 2
    scratch += [pltpu.VMEM((span, group * QB), bf16)] * 2
    return pl.pallas_call(
        functools.partial(attend_back_kernel, last),
        grid_spec=pltpu.PrefetchScalarGridSpec(
            num_scalar_prefetch=1, grid=(4,),
            in_specs=in_specs, out_specs=out_specs, scratch_shapes=scratch,
        ),
        out_shape=out_shape,
        input_output_aliases=aliases,
        compiler_params=params(34),
        cost_estimate=takes(27),
        name="attend_back",
    )(order, *args)


def qkv_back_kernel(order_ref, dq_ref, dkv_ref, wq_ref, wk_ref, wv_ref, send_ref, keep_ref):
    step = pl.program_id(0)
    half = pl.num_programs(0) // 2
    kc = wk_ref.shape[1]
    total = (
        mm(dq_ref[...], wq_ref[...], NT)
        + mm(dkv_ref[:, :kc], wk_ref[...], NT)
        + mm(dkv_ref[:, kc:], wv_ref[...], NT)
    ).astype(bf16)

    @pl.when(step < half)
    def _():
        send_ref[...] = total

    @pl.when(step >= half)
    def _():
        keep_ref[...] = total


def qkv_back_call(order, dq, dkv, wq, wk, wv):
    rows, width = dq.shape[0], wq.shape[0]
    steps = order.shape[0]
    rb = rows // steps
    half = steps // 2
    whole = lambda shape: pl.BlockSpec(shape, lambda s, o: (0,) * len(shape))
    return pl.pallas_call(
        qkv_back_kernel,
        grid_spec=pltpu.PrefetchScalarGridSpec(
            num_scalar_prefetch=1, grid=(steps,),
            in_specs=[
                pl.BlockSpec((rb, dq.shape[1]), lambda s, o: (o[s], 0)),
                pl.BlockSpec((rb, dkv.shape[1]), lambda s, o: (o[s], 0)),
                whole(wq.shape), whole(wk.shape), whole(wv.shape),
            ],
            out_specs=[
                pl.BlockSpec((rb, width), lambda s, o: (jnp.minimum(s, half - 1), 0)),
                pl.BlockSpec((rb, width), lambda s, o: (jnp.maximum(s - half, 0), 0)),
            ],
        ),
        out_shape=[jax.ShapeDtypeStruct((rows // 2, width), bf16)] * 2,
        compiler_params=params(20),
        cost_estimate=takes(9),
        name="qkv_back",
    )(order, dq, dkv, wq, wk, wv)


def dense_grad_kernel(order_ref, n_ref, dq_ref, dkv_ref, db0_ref, db1_ref, db2_ref, db3_ref,
                      heads_ref, normed2_ref, dlog_ref, gain2_ref, gain_ref,
                      wq_ref, wk_ref, wv_ref, out_ref):
    qc, kvc = dq_ref.shape[1], dkv_ref.shape[1]
    quarter = db0_ref.shape[0]
    normed = n_ref[...]
    query, key_value = mm(normed, dq_ref[...], TN), mm(normed, dkv_ref[...], TN)
    out_ref[:, :qc] = query.astype(bf16)
    out_ref[:, qc:qc + kvc] = key_value.astype(bf16)
    first = (
        jnp.sum(query * wq_ref[...].astype(f32), axis=1, keepdims=True)
        + jnp.sum(key_value[:, :kvc // 2] * wk_ref[...].astype(f32), axis=1, keepdims=True)
        + jnp.sum(key_value[:, kvc // 2:] * wv_ref[...].astype(f32), axis=1, keepdims=True)
    )
    wo = None
    for j, db_ref in enumerate((db0_ref, db1_ref, db2_ref, db3_ref)):
        at = pl.multiple_of(order_ref[j] * quarter, quarter)
        part = mm(db_ref[...], heads_ref[pl.ds(at, quarter), :], TN)
        wo = part if wo is None else wo + part
    out_ref[:, qc + kvc:2 * qc + kvc] = wo.astype(bf16)
    router = mm(normed2_ref[...], dlog_ref[...], TN)
    cols = router.shape[0]
    column = lambda row: jnp.transpose(jnp.broadcast_to(row.astype(f32), (8, cols)))[:, :1]
    pad = out_ref.shape[1] - (2 * qc + kvc) - router.shape[1] - 2
    out_ref[:, 2 * qc + kvc:] = jnp.concatenate(
        [router, column(gain2_ref[...]), first / column(gain_ref[...]), jnp.zeros((cols, pad), f32)],
        axis=1,
    ).astype(bf16)


def dense_grad_call(order, normed1, dq, dkv, dbs, heads, normed2, d_logits, gain2, gain, ws):
    rows, width = normed1.shape
    qc, kvc = dq.shape[1], dkv.shape[1]
    cols = width // 6
    lanes = 2 * qc + kvc + -(-(d_logits.shape[1] + 2) // 128) * 128
    whole = lambda a: pl.BlockSpec(a.shape, lambda s, o: (0, 0))
    block = lambda a: pl.BlockSpec((a.shape[0], cols), lambda s, o: (0, s))
    lines = lambda a: pl.BlockSpec((cols, a.shape[1]), lambda s, o: (s, 0))
    return pl.pallas_call(
        dense_grad_kernel,
        grid_spec=pltpu.PrefetchScalarGridSpec(
            num_scalar_prefetch=1,
            grid=(6,),
            in_specs=[block(normed1), whole(dq), whole(dkv), *map(block, dbs), whole(heads),
                      block(normed2), whole(d_logits), block(gain2), block(gain),
                      *map(lines, ws)],
            out_specs=pl.BlockSpec((cols, lanes), lambda s, o: (s, 0)),
        ),
        out_shape=jax.ShapeDtypeStruct((width, lanes), bf16),
        compiler_params=params(36),
        cost_estimate=takes(13),
        name="dense_grad",
    )(order, normed1, dq, dkv, *dbs, heads, normed2, d_logits, gain2, gain, *ws)


def expert_kernel(pieces, cap, experts, base_ref, *refs):
    sources = len(pieces)
    x_refs = []
    for n in pieces:
        x_refs.append(refs[:n])
        refs = refs[n:]
    c_refs = []
    for n in pieces:
        c_refs.append(refs[:n])
        refs = refs[n:]
    router_ref, wg_ref, wu_ref, wd_ref = refs[:4]
    refs = refs[-(4 * sources + 5 + 5):]
    out_refs, refs = refs[:2 * sources], refs[2 * sources:]
    back_refs, refs = refs[:2 * sources], refs[2 * sources:]
    (xs_ref, cs_ref, act_ref, dg_ref, du_ref,
     mix_ref, rank_ref, dmix_ref, so_ref, sd_ref) = refs
    e = pl.program_id(0)
    local = pl.num_programs(0)
    quarter = sum(x_ref.shape[0] for x_ref in x_refs[0])
    half = quarter // 2
    extra = sum(c_ref.shape[0] for c_ref in c_refs[0]) - quarter
    slots = so_ref.shape[1]
    base = base_ref[0]

    @pl.when(e == 0)
    def _():
        for s in range(sources):
            end = c_refs[s][-1]
            tail = end[end.shape[0] - extra:, :].astype(f32)
            rank = jnp.concatenate(
                [tail[:, j * quarter:(j + 1) * quarter] for j in range(-(-experts // extra))],
                axis=0,
            )[:experts].astype(i32)
            rank_ref[s] = rank
            logits = jnp.concatenate(
                [mm(router_ref[...], x_ref[...], NT) for x_ref in x_refs[s]], axis=1
            )
            chosen = rank >= 0
            logits = jnp.where(chosen, logits, NEG)
            top = jnp.max(logits, axis=0, keepdims=True)
            ex = jnp.where(chosen, jnp.exp(logits - top), 0.0)
            mix_ref[s] = ex / jnp.sum(ex, axis=0, keepdims=True)

    slot_row = lax.broadcasted_iota(i32, (cap, quarter), 0)
    picks, mixes = [], []
    for s in range(sources):
        hot = slot_row == rank_ref[s, pl.ds(base + e, 1), :]
        pick = jnp.where(hot, 1.0, 0.0)
        picks.append(pick)
        mixes.append(jnp.sum(pick * mix_ref[s, pl.ds(base + e, 1), :], axis=1, keepdims=True))
        pick = pick.astype(bf16)
        n = quarter // pieces[s]
        xs_ref[0, s * cap:(s + 1) * cap, :] = sum(
            mm(pick[:, j * n:(j + 1) * n], x_ref[...]) for j, x_ref in enumerate(x_refs[s])
        ).astype(bf16)
        cs_ref[0, s * cap:(s + 1) * cap, :] = sum(
            mm(pick[:, j * n:(j + 1) * n], c_ref[:n, :]) for j, c_ref in enumerate(c_refs[s])
        ).astype(bf16)
    mix = jnp.concatenate(mixes, axis=0)
    xs, cs = xs_ref[0], cs_ref[0]
    gate, up = mm(xs, wg_ref[0]), mm(xs, wu_ref[0])
    d_act = mm(cs, wd_ref[0], NT)
    sig = jax.nn.sigmoid(gate)
    silu = gate * sig
    act = silu * up
    d_mix = jnp.sum(act * d_act, axis=1, keepdims=True)
    for s in range(sources):
        dmix_ref[s, pl.ds(e, 1), :] = jnp.sum(
            picks[s] * d_mix[s * cap:(s + 1) * cap], axis=0, keepdims=True
        )
    d_act = d_act * mix
    act = (act * mix).astype(bf16)
    du = (d_act * silu).astype(bf16)
    dg = (d_act * up * sig * (1.0 + gate * (1.0 - sig))).astype(bf16)
    act_ref[0], du_ref[0], dg_ref[0] = act, du, dg
    so = mm(act, wd_ref[0]).astype(bf16)
    sd = (mm(dg, wg_ref[0], NT) + mm(du, wu_ref[0], NT)).astype(bf16)
    at = pl.multiple_of(e * cap, 16)
    for s in range(sources):
        so_ref[s, pl.ds(at, cap), :] = so[s * cap:(s + 1) * cap]
        sd_ref[s, pl.ds(at, cap), :] = sd[s * cap:(s + 1) * cap]

    @pl.when(e == local - 1)
    def _():
        count = slots // cap
        col = lax.broadcasted_iota(i32, (quarter, slots), 1)
        for s in range(sources):
            rows = [rank_ref[s, pl.ds(base + j, 1), :] for j in range(count)]
            rows = [jnp.where(r >= 0, r + j * cap, -1) for j, r in enumerate(rows)]
            rows += [jnp.full((1, quarter), -1, i32)] * (-count % 8)
            back = jnp.transpose(jnp.concatenate(rows, axis=0))
            hot = None
            for j in range(count):
                this = back[:, j:j + 1] == col
                hot = this if hot is None else hot | this
            pick = jnp.where(hot, 1.0, 0.0).astype(bf16)
            for j in range(2):
                part = pick[j * half:(j + 1) * half]
                out_refs[2 * s + j][...] = mm(part, so_ref[s]).astype(bf16)
                back_refs[2 * s + j][:half, :] = mm(part, sd_ref[s]).astype(bf16)
            row = lax.broadcasted_iota(i32, (extra, quarter), 0)
            sums = [jnp.zeros((extra, quarter), f32) for _ in range(x_refs[0][0].shape[1] // quarter)]
            for j in range(count):
                line = dmix_ref[s, j:j + 1, :]
                for piece in range(len(sums)):
                    sums[piece] = jnp.where(row + piece * extra == base + j, line, sums[piece])
            sums = jnp.concatenate(sums, axis=1)
            high = sums.astype(bf16)
            back_refs[2 * s + 1][half:half + extra, :] = high
            back_refs[2 * s + 1][half + extra:, :] = (sums - high.astype(f32)).astype(bf16)


def expert_call(base, xs, cs, router_t, wg, wu, wd, cap, at, of, held=None):
    sources = len(xs)
    experts = router_t.shape[0]
    local, width, hidden = wg.shape
    quarter = sum(part.shape[0] for part in xs[0])
    half = quarter // 2
    pieces = tuple(len(parts) for parts in xs)
    extra = sum(part.shape[0] for part in cs[0]) - quarter
    xs = [part for parts in xs for part in parts]
    cs = [part for parts in cs for part in parts]
    rows = [half] * (2 * sources) + [half, half + 2 * extra] * sources
    sizes = (width, width, hidden, hidden, hidden)
    whole = lambda shape: pl.BlockSpec(shape, lambda e, b: (0,) * len(shape))
    slot_spec = lambda n: pl.BlockSpec((1, sources * cap, n), lambda e, b: (e, at, 0))
    args = [*xs, *cs, router_t, wg, wu, wd]
    in_specs = (
        [whole(a.shape) for a in (*xs, *cs, router_t)]
        + [
            pl.BlockSpec((1, width, hidden), lambda e, b: (e, 0, 0)),
            pl.BlockSpec((1, width, hidden), lambda e, b: (e, 0, 0)),
            pl.BlockSpec((1, hidden, width), lambda e, b: (e, 0, 0)),
        ]
    )
    aliases = {}
    if held is not None:
        aliases = {1 + len(args) + j: 4 * sources + j for j in range(5)}
        args += list(held)
        in_specs += [pl.BlockSpec(memory_space=pl.ANY)] * 5
    outs = pl.pallas_call(
        functools.partial(expert_kernel, pieces, cap, experts),
        grid_spec=pltpu.PrefetchScalarGridSpec(
            num_scalar_prefetch=1,
            grid=(local,),
            in_specs=in_specs,
            out_specs=[whole((n, width)) for n in rows] + [slot_spec(n) for n in sizes],
            scratch_shapes=[
                pltpu.VMEM((sources, experts, quarter), f32),
                pltpu.VMEM((sources, experts, quarter), i32),
                pltpu.VMEM((sources, local, quarter), f32),
                pltpu.VMEM((sources, local * cap, width), bf16),
                pltpu.VMEM((sources, local * cap, width), bf16),
            ],
        ),
        out_shape=[jax.ShapeDtypeStruct((n, width), bf16) for n in rows]
        + [jax.ShapeDtypeStruct((local, of * cap, n), bf16) for n in sizes],
        input_output_aliases=aliases,
        compiler_params=params(60),
        cost_estimate=takes(12 + 11 * sources),
        name="experts",
    )(base, *args)
    halves = lambda a: [(a[2 * s], a[2 * s + 1]) for s in range(sources)]
    return (
        halves(outs[:2 * sources]),
        halves(outs[2 * sources:4 * sources]),
        outs[4 * sources:],
    )


def weight_grad_kernel(order_ref, a_ref, b_ref, send_ref, keep_ref):
    part = mm(a_ref[0], b_ref[0], TN).astype(bf16)
    step = pl.program_id(0)

    @pl.when(step < 2)
    def _():
        send_ref[0, 0] = part

    @pl.when(step >= 2)
    def _():
        keep_ref[0, 0] = part


def weight_grad_call(order, a, b, cut_last=False):
    local, slots, width = (b if cut_last else a).shape
    cut = width // 4
    part = lambda x: pl.BlockSpec((1, slots, cut), lambda s, e, o: (e, 0, o[s]))
    full = lambda x: pl.BlockSpec((1, slots, x.shape[2]), lambda s, e, o: (e, 0, 0))
    dims = (a.shape[2], cut) if cut_last else (cut, b.shape[2])
    shape = jax.ShapeDtypeStruct((2, local, *dims), bf16)
    return pl.pallas_call(
        weight_grad_kernel,
        grid_spec=pltpu.PrefetchScalarGridSpec(
            num_scalar_prefetch=1,
            grid=(4, local),
            in_specs=[full(a), part(b)] if cut_last else [part(a), full(b)],
            out_specs=[
                pl.BlockSpec(
                    (1, 1, *dims),
                    lambda s, e, o: (jnp.minimum(s, 1), jnp.where(s < 2, e, local - 1), 0, 0),
                ),
                pl.BlockSpec(
                    (1, 1, *dims),
                    lambda s, e, o: (jnp.maximum(s - 2, 0), jnp.where(s < 2, 0, e), 0, 0),
                ),
            ],
        ),
        out_shape=[shape, shape],
        compiler_params=params(20, 2),
        cost_estimate=takes(18),
        name="weight_grad",
    )(order, a, b)


def norm_two_kernel(at_ref, x_ref, keep_ref, came_ref, far_ref, gain_ref, middle_ref, out_ref):
    branch = keep_ref[...].astype(f32) + came_ref[...].astype(f32) + far_ref[...].astype(f32)
    middle = x_ref[...].astype(f32) + branch
    middle_ref[...] = middle
    inv = lax.rsqrt(jnp.mean(middle * middle, axis=-1, keepdims=True) + EPS)
    out_ref[...] = (middle * inv * gain_ref[...].astype(f32)).astype(bf16)


def norm_two_call(t_rank, x, keep, came, far, gain):
    quarter, width = keep.shape
    rb = quarter // 4
    row = pl.BlockSpec((rb, width), lambda s, t: (s, 0))
    return pl.pallas_call(
        norm_two_kernel,
        grid_spec=pltpu.PrefetchScalarGridSpec(
            num_scalar_prefetch=1,
            grid=(4,),
            in_specs=[
                pl.BlockSpec((rb, width), lambda s, t: (4 * t[0] + s, 0)), row, row, row,
                pl.BlockSpec((1, width), lambda s, t: (0, 0)),
            ],
            out_specs=[row, row],
        ),
        out_shape=[
            jax.ShapeDtypeStruct((quarter, width), f32),
            jax.ShapeDtypeStruct((quarter, width), bf16),
        ],
        compiler_params=params(12),
        cost_estimate=takes(3),
        name="norm_two",
    )(t_rank, x, keep, came, far, gain)


def middle_back_kernel(*refs):
    terms, tails, refs = refs[:6], refs[6:9], refs[9:]
    (mix_ref, router_ref, middle_ref, cot_ref, gain_ref,
     dmid_ref, db_ref, dlog_ref, gain2_ref, dl_ref) = refs
    step = pl.program_id(0)
    rb, width = middle_ref.shape
    experts, quarter = mix_ref.shape

    @pl.when(step == 0)
    def _():
        tail = sum(t[...].astype(f32) for t in tails)
        extra = tail.shape[0] // 2
        tail = tail[:extra] + tail[extra:]
        d_mix = jnp.concatenate(
            [tail[:, j * quarter:(j + 1) * quarter] for j in range(-(-experts // extra))], axis=0
        )[:experts]
        mix = mix_ref[...]
        d_logits = mix * (d_mix - jnp.sum(mix * d_mix, axis=0, keepdims=True))
        d_logits = jnp.transpose(d_logits).astype(bf16)
        dlog_ref[...] = d_logits
        dl_ref[...] = d_logits
        gain2_ref[...] = jnp.zeros_like(gain2_ref)

    first = [t[...].astype(f32) for t in terms[:3]]
    second = [t[...].astype(f32) for t in terms[3:]]
    routed = jnp.where(step < pl.num_programs(0) // 2, sum(first), sum(second))
    d_logits = dl_ref[pl.ds(pl.multiple_of(step * rb, rb), rb), :]
    d_normed = routed + mm(d_logits, router_ref[...])
    middle = middle_ref[...]
    inv = lax.rsqrt(jnp.mean(middle * middle, axis=-1, keepdims=True) + EPS)
    gain2_ref[...] += jnp.sum(d_normed * middle * inv, axis=0, keepdims=True)
    scaled = d_normed * gain_ref[...].astype(f32)
    d_middle = (
        cot_ref[...].astype(f32)
        + inv * scaled
        - middle * (inv * inv * inv * jnp.mean(scaled * middle, axis=-1, keepdims=True))
    )
    dmid_ref[...] = d_middle
    db_ref[...] = d_middle.astype(bf16)


def middle_back_call(terms, mix_t, router_t, middle, cotangent, gain):
    quarter, width = middle.shape
    experts = mix_t.shape[0]
    half = quarter // 2
    tail = terms[0][1].shape[0] - half
    rb = half // 4
    row = pl.BlockSpec((rb, width), lambda s: (s, 0))
    low = pl.BlockSpec((rb, width), lambda s: (jnp.minimum(s, 3), 0))
    high = pl.BlockSpec((rb, width), lambda s: (jnp.maximum(s - 4, 0), 0))
    end = pl.BlockSpec((tail, width), lambda s: (half // tail, 0))
    whole = lambda shape: pl.BlockSpec(shape, lambda s: (0,) * len(shape))
    firsts, seconds = [t[0] for t in terms], [t[1] for t in terms]
    return pl.pallas_call(
        middle_back_kernel,
        grid=(8,),
        in_specs=[low] * 3 + [high] * 3 + [end] * 3
        + [whole((experts, quarter)), whole((experts, width)), row, row, whole((1, width))],
        out_specs=[row, row, whole((quarter, experts)), whole((1, width))],
        out_shape=[
            jax.ShapeDtypeStruct((quarter, width), f32),
            jax.ShapeDtypeStruct((quarter, width), bf16),
            jax.ShapeDtypeStruct((quarter, experts), bf16),
            jax.ShapeDtypeStruct((1, width), f32),
        ],
        scratch_shapes=[pltpu.VMEM((quarter, experts), bf16)],
        compiler_params=params(16),
        cost_estimate=takes(7),
        name="middle_back",
    )(*firsts, *seconds, *seconds, mix_t, router_t, middle, cotangent, gain)


def in_first_half():
    return pl.program_id(0) < pl.num_programs(0) // 2


def two_sums_kernel(first, wait_ref, a_ref, b_ref, p0_ref, p1_ref, m0_ref, m1_ref, pa_ref, mb_ref):
    plus = jnp.where(in_first_half(), p0_ref[...], p1_ref[...]).astype(f32)
    minus = jnp.where(in_first_half(), m0_ref[...], m1_ref[...]).astype(f32)
    a, b = a_ref[...].astype(f32), b_ref[...].astype(f32)
    if first:
        a, b = jnp.where(in_first_half(), a, 0.0), jnp.where(in_first_half(), 0.0, b)
    pa_ref[...] = (a + plus).astype(bf16)
    mb_ref[...] = (b + minus).astype(bf16)


def half_specs(rb, width):
    return (
        pl.BlockSpec((rb, width), lambda s, *_: (s, 0)),
        pl.BlockSpec((rb, width), lambda s, *_: (jnp.minimum(s, 3), 0)),
        pl.BlockSpec((rb, width), lambda s, *_: (jnp.maximum(s - 4, 0), 0)),
    )


def two_sums_call(wait, a, b, plus, minus, first):
    rows, width = 2 * plus[0].shape[0], plus[0].shape[1]
    row, low, high = half_specs(rows // 8, width)
    return pl.pallas_call(
        functools.partial(two_sums_kernel, first),
        grid_spec=pltpu.PrefetchScalarGridSpec(
            num_scalar_prefetch=1,
            grid=(8,),
            in_specs=[low if first else row, high if first else row, low, high, low, high],
            out_specs=[row, row],
        ),
        out_shape=[jax.ShapeDtypeStruct((rows, width), bf16)] * 2,
        compiler_params=params(10),
        cost_estimate=takes(4),
        name="two_sums",
    )(wait.astype(i32)[None], a, b, *plus, *minus)


def layer_out_kernel(middle_ref, first_ref, second_ref, a_ref, b_ref, out_ref):
    own = jnp.where(in_first_half(), first_ref[...], second_ref[...]).astype(f32)
    out_ref[...] = (
        middle_ref[...] + own + a_ref[...].astype(f32) + b_ref[...].astype(f32)
    ).astype(bf16)


def layer_out_call(middle, own, a, b):
    quarter, width = middle.shape
    row, low, high = half_specs(quarter // 8, width)
    return pl.pallas_call(
        layer_out_kernel,
        grid=(8,),
        in_specs=[row, low, high, row, row],
        out_specs=row,
        out_shape=jax.ShapeDtypeStruct((quarter, width), bf16),
        compiler_params=params(10),
        cost_estimate=takes(4),
        name="layer_out",
    )(middle, *own, a, b)


def input_back_kernel(at_ref, keep_ref, came_ref, far_ref, dmid_ref, x_ref, gain_ref, out_ref):
    d_normed = keep_ref[...].astype(f32) + came_ref[...].astype(f32) + far_ref[...].astype(f32)
    x = x_ref[...].astype(f32)
    inv = lax.rsqrt(jnp.mean(x * x, axis=-1, keepdims=True) + EPS)
    scaled = d_normed * gain_ref[...].astype(f32)
    out_ref[...] = (
        dmid_ref[...]
        + inv * scaled
        - x * (inv * inv * inv * jnp.mean(scaled * x, axis=-1, keepdims=True))
    )


def input_back_call(t_rank, keep, came, far, d_middle, x, gain):
    quarter, width = d_middle.shape
    rb = quarter // 8
    row = pl.BlockSpec((rb, width), lambda s, t: (s, 0))
    behind = pl.BlockSpec((rb, width), lambda s, t: (8 + s, 0))
    return pl.pallas_call(
        input_back_kernel,
        grid_spec=pltpu.PrefetchScalarGridSpec(
            num_scalar_prefetch=1,
            grid=(8,),
            in_specs=[
                behind, behind, row, row,
                pl.BlockSpec((rb, width), lambda s, t: (8 * t[0] + s, 0)),
                pl.BlockSpec((1, width), lambda s, t: (0, 0)),
            ],
            out_specs=row,
        ),
        out_shape=jax.ShapeDtypeStruct((quarter, width), f32),
        compiler_params=params(10),
        cost_estimate=takes(6),
        name="input_back",
    )(t_rank, keep, came, far, d_middle, x, gain)


def ring_of(n):
    return list(range(0, n, 2)) + list(range(n - 1, 0, -2))


def index_at(place, n):
    return jnp.where(place < n // 2, 2 * place, 2 * n - 1 - 2 * place)


def ring_moves(n):
    ring = ring_of(n)
    ahead = [(ring[p], ring[(p + 1) % n]) for p in range(n)]
    return ahead, [(b, a) for a, b in ahead]


def add_low(a, b, wait=0.0):
    return (a.astype(f32) + jnp.asarray(b).astype(f32) + wait).astype(bf16)


class RingSum:

    def __init__(self, own, parts, n):
        self.own, self.parts, self.half = own, parts, n // 2
        self.ways = ring_moves(n)
        self.long, self.short = [None, None], [None, None]
        self.rounds = 0

    def term(self, distance, way, half):
        if distance == self.half:
            return self.parts[-1][0][half]
        return self.parts[distance - 1][1 - way][half]

    def round(self, wait=0.0):
        r = self.rounds
        self.rounds += 1
        sums = []
        for held, hop, distance, turn in (
            (self.short, r, self.half - 1 - r, 1),
            (self.long, r - 1, self.half + 1 - r, 0),
        ):
            if hop < 0 or distance < 1:
                continue
            for way in range(2):
                t = self.term(distance, way, (way + turn) % 2)
                if hop > 0:
                    t = add_low(held[way], t, wait)
                    sums.append(t)
                held[way] = lax.ppermute(t, "dp", self.ways[way])
        return sums

    def terms(self):
        a, b = self.long, self.short
        return [tuple(self.own), (a[0], b[0]), (b[1], a[1])]


CORE = [(0, 1), (1, 0), (2, 3), (3, 2)]
CHIP = [(0, 2), (2, 0), (1, 3), (3, 1)]


def to_core(a):
    return lax.ppermute(a, "tensor", CORE)


def to_chip(a):
    return lax.ppermute(a, "tensor", CHIP)


def zero_of(a):
    while a.ndim > 2:
        a = a[0]
    return jnp.minimum(jnp.abs(a[0, 0].astype(f32)), 0.0)


def mark(a):
    while a.ndim > 2:
        a = a[0]
    return zero_of(a)


def after(first, then):
    return lax.optimization_barrier((then, first))[0]


def per_device(layer_input, segments, routes, norm1_gain, w_query, w_key, w_value, w_output,
               norm2_gain, router, w_gate, w_up, w_down, cotangent, n_dp):
    tokens_dev, width = layer_input.shape
    quarter, top_count = routes.shape
    experts = router.shape[1]
    local = w_gate.shape[0]
    cap = quarter * top_count * 5 // (4 * experts)
    hidden = w_gate.shape[2]
    t_rank = lax.axis_index("tensor")
    d_rank = lax.axis_index("dp")
    place = jnp.where(d_rank % 2 == 0, d_rank // 2, n_dp - 1 - d_rank // 2)
    ringed = n_dp in (4, 6, 8)
    cos, sin = rope_tables()

    hot_t = jnp.any(
        routes.T[:, None, :] == jnp.arange(experts, dtype=i32)[None, :, None], axis=0
    )
    before = (jnp.arange(quarter)[:, None] < jnp.arange(quarter)[None, :]).astype(bf16)
    rank_t = jnp.dot(hot_t.astype(bf16), before, preferred_element_type=f32)
    rank_t = jnp.where(hot_t, rank_t, -1.0).astype(bf16)
    per_row = width // quarter
    extra = 16 * -(-experts // (16 * per_row))
    rank_rows = jnp.concatenate(
        [rank_t, jnp.full((extra * per_row - experts, quarter), -1.0, bf16)], axis=0
    ).reshape(per_row, extra, quarter)
    rank_rows = jnp.concatenate([rank_rows[j] for j in range(per_row)], axis=1)
    payload = jnp.concatenate([cotangent, rank_rows], axis=0)
    router_t = router.T
    ahead, behind = ring_moves(n_dp)
    zero = jnp.zeros((), i32)
    own_at = t_rank.astype(i32)[None]
    mate, other, cross = t_rank ^ 1, t_rank ^ 2, t_rank ^ 3
    quarters = jnp.stack([cross, mate, other, t_rank]).astype(i32)
    pairs_of = lambda *ts: jnp.stack([2 * t + j for t in ts for j in range(2)]).astype(i32)

    if ringed:
        a = b = payload
        grads_from = []
        for _ in range(n_dp // 2 - 1):
            a, b = lax.ppermute(a, "dp", ahead), lax.ppermute(b, "dp", behind)
            grads_from.append(((a,), (b,)))
        stage = [after(g, zero) for g in grads_from]
    else:
        stage = [zero] * 3
    normed1, q, k, v, kt = qkv_call(
        layer_input, after(payload, norm1_gain[None, :]), w_query, w_key, w_value, cos, sin
    )
    seg_col, seg_row = segments[:, None], segments[None, :]
    heads, lse, send_a, keep_a = attend_call(
        pairs_of(cross, other), q, k, v, seg_col, seg_row, w_output
    )
    if ringed:
        send_a, grads_from[0] = lax.optimization_barrier((send_a, grads_from[0]))
    sum_a = add_low(keep_a, to_core(send_a))
    far = to_chip(sum_a)
    heads, lse, send_b, keep_b = attend_call(
        after(sum_a, pairs_of(mate, t_rank)),
        q, k, v, seg_col, seg_row, w_output, held=(heads, lse),
    )
    came_b = jnp.concatenate([to_core(send_b[:QB]), to_core(send_b[QB:])], axis=0)
    middle, normed2 = norm_two_call(
        own_at + stage[1], layer_input, keep_b, came_b, far, norm2_gain[None, :]
    )

    base = (d_rank * local).astype(i32)[None]
    run = lambda base, xs, cs, at, of, held: expert_call(
        base, xs, cs, router_t, w_gate, w_up, w_down, cap, at, of, held
    )

    def own_mixing(rows):
        return jax.nn.softmax(jnp.where(hot_t, mm(router_t, rows, NT), -jnp.inf), axis=0)

    def core_sum(parts, wait):
        send, keep = parts
        came = to_core(send)
        away = add_low(keep[0], came[0], wait)
        return keep[1], came[1], away

    def chip_sum(sums, wait):
        keep, came, away = sums
        return keep.astype(f32) + came.astype(f32) + to_chip(away).astype(f32) + wait

    if ringed:
        step = lambda rows, way: (lax.ppermute(rows, "dp", way),)
        xs = [step(normed2, ahead), step(normed2, behind)]
        (out_own,), (back_own,), held = run(base, [(normed2,)], [(payload,)], n_dp - 1, n_dp, None)
        outs, backs, last = [], [], out_own
        cut = payload.shape[0] // 32 * 16
        for j in range(n_dp // 2):
            cs = grads_from[j]
            if j < n_dp // 2 - 1:
                at = j
                (a,), (b,) = after(last, xs)
                if j < n_dp // 2 - 2:
                    later = [step(a, ahead), step(b, behind)]
                else:
                    later = [step(a[:quarter // 2], ahead) + step(b[quarter // 2:], behind)]
            else:
                at = n_dp - 2
            if j == n_dp // 2 - 2:
                (a,), (b,) = after(last, grads_from[-1])
                a, b = lax.ppermute(a[:cut], "dp", ahead), lax.ppermute(b[cut:], "dp", behind)
                grads_from.append(((a, b),))
            o, b, held = run(base, xs, cs, at, n_dp, held)
            outs.append(o)
            backs.append(b)
            last, xs = o, later
        back = RingSum(back_own, backs, n_dp)
        back.round()
        sums = back.round(mark(backs[-1][0][0]))
        mix_t = own_mixing(after(sums, normed2))
        grad_of = lambda i, j: weight_grad_call(
            quarters + after(sums, zero), held[i], held[j]
        )
        gate_parts = grad_of(0, 3)
        sums = back.round(mark(gate_parts[1]))
        up_parts = grad_of(0, 4)
        end = mark(up_parts[1])
        sums = back.round(end)
        gate_sum = core_sum(gate_parts, end)
        down_parts = weight_grad_call(
            quarters + after(sums, zero) + zero_of(gate_sum[2]).astype(i32), held[2], held[1], True
        )
        end = mark(down_parts[1])
        sums = back.round(end)
        gate_grad = chip_sum(gate_sum, end)
        gate_done = zero_of(gate_grad)
        routed = back.terms()
    else:
        grads_all = lax.all_gather(payload, "dp", axis=0)
        rows_all = lax.all_gather(normed2, "dp", axis=0)
        halves = lambda a: (a[:quarter // 2], a[quarter // 2:])

        def two(sums, pair_rows):
            x, c = pair_rows
            o, b, held = run(base, [(x[0],), (x[1],)], [(c[0],), (c[1],)], 0, 2, None)
            grads = [
                list(weight_grad_call(quarters, held[i], held[j], i == 2))
                for i, j in ((0, 3), (0, 4), (2, 1))
            ]
            sums = jax.tree.map(lambda t, g: t + g.astype(f32), sums, grads)
            join = lambda a: jnp.stack([jnp.concatenate(h, axis=0) for h in a])
            return sums, (join(o), join(b))

        pairs = lambda a: a.reshape((n_dp // 2, 2) + a.shape[1:])
        none = jnp.zeros((2, local, width // 4, hidden), f32)
        none = [[none] * 2, [none] * 2, [none.transpose(0, 1, 3, 2)] * 2]
        grads, (outs, backs) = lax.scan(
            two, none, (pairs(rows_all), pairs(grads_all))
        )
        gate_parts, up_parts, down_parts = jax.tree.map(lambda a: a.astype(bf16), grads)
        gate_grad = chip_sum(core_sum(gate_parts, 0.0), 0.0)
        gate_done = 0.0
        scatter = lambda a: lax.psum_scatter(
            a.reshape(-1, width), "dp", scatter_dimension=0, tiled=True
        )
        mix_t = own_mixing(normed2)
        empty = jax.tree.map(jnp.zeros_like, halves(scatter(backs)))
        routed = [halves(scatter(backs)), empty, empty]

    d_middle, db_own, d_logits, second_gain_part = middle_back_call(
        routed, mix_t, router_t, middle, cotangent,
        (norm2_gain.astype(f32) + gate_done).astype(bf16)[None, :],
    )

    db_mate = to_core(db_own)
    other_first, other_second = to_chip(db_own[:QB]), to_chip(db_own[QB:])
    common = (q, k, v, kt, seg_row, seg_col, heads, lse)
    if ringed:
        out_a, out_b = after(sums, outs[-1][0])
        out_a, out_b = lax.ppermute(out_a, "dp", ahead), lax.ppermute(out_b, "dp", behind)

        def out_step(a, b, j, wait):
            minus, plus = outs[j - 1]
            a, b = two_sums_call(wait, a, b, plus, minus, j == n_dp // 2 - 1)
            return lax.ppermute(a, "dp", ahead), lax.ppermute(b, "dp", behind), (a, b)

        steps = list(range(n_dp // 2 - 1, 0, -1))
    else:
        out_own = halves(scatter(outs))
        out_a = out_b = jnp.zeros((quarter, width), bf16)
        out_step = lambda a, b, j, wait: (a, b, zero)
        steps = [0, 0, 0]
    out_a, out_b, sums = out_step(out_a, out_b, steps[0], zero_of(db_own))
    dq, dk, dv = attend_back_call(
        pairs_of(t_rank, mate) + after(sums, zero) + zero_of(other_first).astype(i32), *common, db_own, db_mate, w_output, cos, sin
    )
    end = mark(dq)
    db_other = add_low(jnp.concatenate([other_first, other_second], axis=0), end)
    up_sum = core_sum(up_parts, end)
    out_a, out_b, sums = out_step(out_a, out_b, steps[1], end)
    db_cross = to_core(db_other)
    dq, dkv = attend_back_call(
        pairs_of(other, cross) + after(sums, zero)
        + zero_of(up_sum[2]).astype(i32),
        *common, db_other, db_cross, w_output,
        cos, sin, held=(dq, dk, dv),
    )
    up_grad = chip_sum(up_sum, zero_of(dkv))
    packed_dense = dense_grad_call(
        jnp.stack([t_rank, mate, other, cross]).astype(i32)
        + (zero_of(out_a) + zero_of(out_b)).astype(i32),
        normed1, dq, dkv, (db_own, db_mate, db_other, db_cross), heads, normed2, d_logits,
        second_gain_part, norm1_gain[None, :], (w_query, w_key, w_value),
    )
    down_sum = core_sum(down_parts, zero_of(packed_dense))
    send, keep = qkv_back_call(
        pairs_of(cross, mate, other, t_rank) + after(packed_dense, zero)
        + zero_of(up_grad).astype(i32),
        dq, dkv, w_query, w_key, w_value,
    )
    came = to_core(send)
    for j in steps[2:]:
        out_a, out_b, sums = out_step(out_a, out_b, j, mark(keep))
    sum_in = add_low(
        keep[:quarter], came[:quarter], zero_of(sums[0]) if ringed else 0.0
    )
    far = to_chip(sum_in)
    down_grad = chip_sum(down_sum, zero_of(sum_in))

    input_grad = input_back_call(
        own_at, keep, came, far, d_middle, layer_input, norm1_gain[None, :]
    )

    dense_sum = lax.psum_scatter(
        packed_dense, "dp", scatter_dimension=0, tiled=True
    ).astype(f32)
    q_cols, kv_cols = w_query.shape[1], w_key.shape[1]
    query_grad = dense_sum[:, :q_cols]
    key_grad = dense_sum[:, q_cols:q_cols + kv_cols]
    value_grad = dense_sum[:, q_cols + kv_cols:q_cols + 2 * kv_cols]
    cols = 2 * (q_cols + kv_cols)
    output_grad = jnp.transpose(dense_sum[:, q_cols + 2 * kv_cols:cols])
    rows = width // n_dp
    small = dense_sum[:, cols:cols + experts + 2] + zero_of(input_grad)
    small = small + to_core(small)
    small = small + to_chip(small)
    small = lax.dynamic_slice_in_dim(small, t_rank * (rows // 4), rows // 4)

    layer_out = layer_out_call(middle, out_own, out_a, out_b)
    return (
        layer_out,
        input_grad,
        small[:, experts + 1],
        query_grad,
        key_grad,
        value_grad,
        output_grad,
        small[:, experts],
        small[:, :experts],
        gate_grad,
        up_grad,
        down_grad,
    )


def solution(mesh):
    both = ("dp", "tensor")
    return jax.shard_map(
        functools.partial(per_device, n_dp=mesh.shape["dp"]),
        mesh=mesh,
        in_specs=(
            P("dp", None), P("dp"), P(both, None), P(),
            P(None, "tensor"), P(None, "tensor"), P(None, "tensor"), P("tensor", None),
            P(), P(), P("dp", None, None), P("dp", None, None), P("dp", None, None),
            P(both, None),
        ),
        out_specs=(
            P(both, None), P(both, None), P(both), P("dp", "tensor"), P("dp", "tensor"),
            P("dp", "tensor"), P("tensor", "dp"), P(both), P(both, None),
            P("dp", "tensor", None), P("dp", "tensor", None), P("dp", None, "tensor"),
        ),
        check_vma=False,
    )
```
